256 devices in a mesh: grp: 2 (over z_hi), vocab: 32 (over y, x, core), tok: 4 (over z_lo).
Axes of the slice: x: 4, y: 4, z: 8 (z_hi: 2, z_lo: 4; z = z_hi * 4 + z_lo), core: 2. Of those that a mesh axis runs over, the one named last changes fastest.
Arguments:
- hidden: bfloat16 [2, 512, 4096], P('grp', 'tok', 'vocab'), may hold values from -24 to 24
- head_weight: bfloat16 [2, 151936, 4096], P('grp', ('vocab', 'tok')), may hold values from -0.703125 to 0.703125
- labels: int32 [512], replicated, may hold values from 0 to 151935
- loss_mask: int32 [512], replicated, may hold values 0 or 1
Outputs:
- head_input_grads: bfloat16 [512, 4096], P(('grp', 'tok'), 'vocab')
- token_loss: float32 [512], replicated
- log_norms: float32 [2, 512], replicated
The draws below stay inside these ranges and needn't reach their ends.
All inputs are finite; a program needn't handle non-finite values.
Results may differ from the reference program's by a relative error of at most 0.0012.
The reference program's roundings to bfloat16 on the way count: a program that leaves them out, or rounds other values in their place, can miss the bound.
Values may be sent and summed in bfloat16 or wider, within the bound.
No kernel may reach another device: no remote copies, remote signals or barrier semaphores. Data moves between devices by JAX's collectives and lax.ppermute only.
A program may use at most 128 MiB of HBM per device.

```python
import math
import jax
import jax.numpy as jnp
import numpy as np
from jax import lax

D = 4096
V = 151936
TOKENS = 512


aligned_count = 4


def drawn_pattern(key):
    key = jax.random.fold_in(key, 5)
    sign_key, token_key, word_key, strength_key, height_key, gap_key = jax.random.split(key, 6)
    signs = jax.random.randint(sign_key, (2, aligned_count, D), 0, 2).astype(jnp.float32) * 2.0 - 1.0
    token_stride = TOKENS // aligned_count
    word_stride = V // aligned_count
    token_pos = (jnp.arange(aligned_count, dtype=jnp.int32)[None, :] * token_stride + jax.random.randint(token_key, (2, aligned_count), 0, token_stride)).astype(jnp.int32)
    word_pos = (jnp.arange(aligned_count, dtype=jnp.int32)[None, :] * word_stride + jax.random.randint(word_key, (2, aligned_count), 0, word_stride - 1)).astype(jnp.int32)
    strength = jax.random.uniform(strength_key, (2, aligned_count), jnp.float32, 1.5, 5.0)
    height = jax.random.uniform(height_key, (2, aligned_count), jnp.float32, 1.5, 3.0)
    gap = jax.random.uniform(gap_key, (2, aligned_count), jnp.float32, 1.0, 3.0)
    return (signs, token_pos, word_pos, strength, height, gap)


def draw_hidden(key, part):
    signs, token_pos, word_pos, strength, height, gap = drawn_pattern(key)
    key = jax.random.fold_in(key, 11)
    normal_key, scale_key = jax.random.split(key)
    values = jax.random.truncated_normal(normal_key, -6.0, 6.0, (2, TOKENS, D), jnp.float32)
    row_scale = jnp.exp(jax.random.uniform(scale_key, (2, TOKENS, 1), jnp.float32, math.log(0.06), math.log(0.24)))
    values = values * row_scale
    group_ids = jnp.arange(2, dtype=jnp.int32)[:, None]
    values = values.at[group_ids, token_pos].set(strength[:, :, None] * signs)
    values = jnp.clip(values, -24.0, 24.0)
    return values.astype(jnp.bfloat16)


def draw_head_weight(key, part):
    signs, token_pos, word_pos, strength, height, gap = drawn_pattern(key)
    key = jax.random.fold_in(key, 23)
    base_key, scale_key, mean_key = jax.random.split(key, 3)
    row_scale = jnp.exp(jax.random.uniform(scale_key, (2, V, 1), jnp.float32, 0.0, math.log(9.0)))
    base_draw = jax.random.truncated_normal(base_key, -4.0, 4.0, (2, V, D), jnp.float32)
    common_row = jax.random.truncated_normal(mean_key, -3.0, 3.0, (2, 1, D), jnp.float32)
    values = base_draw * row_scale + common_row
    group_ids = jnp.arange(2, dtype=jnp.int32)[:, None]
    second_height = height - gap / (strength * math.sqrt(D))
    values = values.at[group_ids, word_pos].set(height[:, :, None] * signs)
    values = values.at[group_ids, word_pos + 1].set(second_height[:, :, None] * signs)
    return (values / math.sqrt(D)).astype(jnp.bfloat16)


def place_ends(array, own_key, smallest, high):
    longest = array.shape.index(max(array.shape))
    spots = []
    for shift in (0, 1):
        where = [jax.random.randint(jax.random.fold_in(own_key, axis), (), 0, length) for axis, length in enumerate(array.shape)]
        where[longest] = (where[longest] + shift) % array.shape[longest]
        spots.append(tuple(where))
    return array.at[spots[0]].set(smallest).at[spots[1]].set(high)


def ranked_wide(own_key, shape, count, slope):
    loads = [min(1 << octave, count + 1 - (1 << octave)) * (1 << 20) // math.isqrt((1 << octave) ** slope) + 1 for octave in range((count + 1).bit_length()) if 1 << octave <= count]
    spread = 1 + sum(loads) // (1 << 30)
    table = np.cumsum(np.array([max(1, weight // spread) for weight in loads]))
    pick = jax.random.randint(jax.random.fold_in(own_key, 1), shape, 0, int(table[len(loads) - 1]))
    start = jnp.left_shift(1, jnp.searchsorted(jnp.asarray(table, jnp.int32), pick, side="right").astype(jnp.int32))
    rank = start - 1 + jax.random.randint(jax.random.fold_in(own_key, 4), shape, 0, 1 << 30) % jnp.minimum(start, count + 1 - start)
    return jax.random.permutation(jax.random.fold_in(own_key, 2), count)[rank].astype(jnp.int32)


def setup_inputs(seed: int = 0) -> dict:
    seeds = jax.random.split(jax.random.key(seed), 5)
    return {
        "hidden": draw_hidden(jax.random.fold_in(seeds[4], 71), 0),
        "head_weight": draw_head_weight(jax.random.fold_in(seeds[4], 71), 0),
        "labels": place_ends(ranked_wide(seeds[2], (TOKENS,), V, 2), jax.random.fold_in(seeds[2], 3), 0, V - 1).astype(jnp.int32),
        "loss_mask": place_ends((jax.random.randint(seeds[3], (TOKENS,), 0, 4) < 3).astype(jnp.int32), jax.random.fold_in(seeds[3], 1), 0, 1),
    }


def group_logits(hidden, head_weight, group_index):
    scores = jnp.dot(head_weight[group_index], hidden[group_index].T, preferred_element_type=jnp.float32)
    return lax.optimization_barrier(scores.astype(jnp.bfloat16)).astype(jnp.float32)


def reference(hidden, head_weight, labels, loss_mask):
    teacher_z = group_logits(hidden, head_weight, 0)
    student_z = group_logits(hidden, head_weight, 1)
    teacher_norm = jax.nn.logsumexp(teacher_z, axis=0)
    student_norm = jax.nn.logsumexp(student_z, axis=0)
    teacher_logp = teacher_z - teacher_norm
    student_logp = student_z - student_norm
    teacher_prob = jnp.exp(teacher_logp)
    student_prob = jnp.exp(student_logp)
    diverge = jnp.sum(teacher_prob * (teacher_logp - student_logp), axis=0)
    positions = jnp.arange(TOKENS, dtype=jnp.int32)
    label_logit = student_z[labels, positions]
    label_hit = (jnp.arange(V, dtype=jnp.int32)[:, None] == labels[None, :]).astype(jnp.float32)
    weight_mask = loss_mask.astype(jnp.float32)
    student_grad = ((2.0 * student_prob - teacher_prob - label_hit) * weight_mask).astype(jnp.bfloat16)
    grad_student = jnp.dot(student_grad.T, head_weight[1], preferred_element_type=jnp.float32)
    token_loss = weight_mask * (diverge + student_norm - label_logit)
    return grad_student.astype(jnp.bfloat16), token_loss, jnp.stack([teacher_norm, student_norm])
```

```python
import functools
import jax
import jax.numpy as jnp
from jax import lax
from jax.experimental import pallas as pl
from jax.experimental.pallas import tpu as pltpu
from jax.sharding import Mesh, PartitionSpec as P

BF16 = jnp.bfloat16
F32 = jnp.float32
VMEM_LIMIT = 48 * 1024 * 1024


def shifts(x, axis, step):
    size = lax.axis_size(axis)
    return lax.ppermute(x, axis, [(i, (i + step) % size) for i in range(size)])


def student_shifts(x, axis, step):
    size = lax.axis_size(axis)
    return lax.ppermute(
        x, ("grp", axis), [(size + i, size + (i + step) % size) for i in range(size)]
    )


def gathered(x, axis):
    return [x] + [shifts(x, axis, k) for k in range(1, lax.axis_size(axis))]


def kernel_call(kernel, out_shape, scalars, *arrays, scratch=()):
    many = pl.BlockSpec(memory_space=pltpu.VMEM)
    return pl.pallas_call(
        kernel,
        out_shape=out_shape,
        in_specs=[pl.BlockSpec(memory_space=pltpu.SMEM)] + [many] * len(arrays),
        out_specs=jax.tree.map(lambda _: many, out_shape),
        scratch_shapes=list(scratch),
        compiler_params=pltpu.CompilerParams(vmem_limit_bytes=VMEM_LIMIT),
    )(scalars, *arrays)


def order_tok_kernel(place_ref, p0, p1, p2, p3, o0, o1, o2, o3, held):
    me = place_ref[3]
    for k, piece in enumerate((p0, p1, p2, p3)):
        held[lax.rem(me + 4 - k, 4)] = piece[...]
    for j, out in enumerate((o0, o1, o2, o3)):
        out[...] = held[j]


def join_features_kernel(place_ref, u0, u1, u2, u3, v0, v1, v2, v3, other, out):
    y, x, core = place_ref[0], place_ref[1], place_ref[2]
    rows = u0.shape[1]
    wide = u0.shape[2]
    for ky in range(4):
        for kx in range(4):
            chip = lax.rem(y + 4 - ky, 4) * 4 + lax.rem(x + 4 - kx, 4)
            own = pl.ds(pl.multiple_of((chip * 2 + core) * wide, wide), wide)
            sib = pl.ds(pl.multiple_of((chip * 2 + 1 - core) * wide, wide), wide)
            out[:rows, own] = (u0, u1, u2, u3)[ky][kx]
            out[rows:, own] = (v0, v1, v2, v3)[kx][ky]
            out[:rows, sib] = other[ky, kx]
            out[rows:, sib] = other[4 + kx, ky]


def split_features_kernel(place_ref, full, keep_x, keep_y, send_x, send_y):
    core = place_ref[2]
    rows = full.shape[0] // 2
    wide = full.shape[1] // 2
    low = full[:, :wide]
    high = full[:, wide:]
    mine = jnp.where(core == 0, low, high)
    theirs = jnp.where(core == 0, high, low)
    keep_x[0, 0] = mine[:rows]
    keep_y[0, 0] = mine[rows:]
    send_x[0, 0] = theirs[:rows]
    send_y[0, 0] = theirs[rows:]


def split_features(place, full):
    tokens, feats = full.shape
    rows, wide = tokens // 2, feats // 32
    x_first = pl.BlockSpec((1, 1, rows, wide), lambda i, p: (i % 4, i // 4, 0, 0))
    y_first = pl.BlockSpec((1, 1, rows, wide), lambda i, p: (i // 4, i % 4, 0, 0))
    part = jax.ShapeDtypeStruct((4, 4, rows, wide), full.dtype)
    return pl.pallas_call(
        split_features_kernel,
        out_shape=[part] * 4,
        grid_spec=pltpu.PrefetchScalarGridSpec(
            num_scalar_prefetch=1,
            grid=(16,),
            in_specs=[
                pl.BlockSpec(
                    (tokens, 2 * wide),
                    lambda i, p: (
                        0,
                        lax.rem(p[0] + i // 4, 4) * 4 + lax.rem(p[1] + i % 4, 4),
                    ),
                )
            ],
            out_specs=[x_first, y_first, x_first, y_first],
        ),
        compiler_params=pltpu.CompilerParams(vmem_limit_bytes=VMEM_LIMIT),
    )(place, full)


def split_rows_kernel(place_ref, a0, a1, a2, a3, b0, b1, b2, b3, o0, o1, o2, o3, held):
    me = place_ref[3]
    half = a0.shape[0]
    rows = o0.shape[0]
    held[:half] = (a0[...] + a1[...]) + (a2[...] + a3[...])
    held[half:] = (b0[...] + b1[...]) + (b2[...] + b3[...])
    for k, out in enumerate((o0, o1, o2, o3)):
        start = pl.multiple_of(lax.rem(me + k, 4) * rows, rows)
        out[...] = held[pl.ds(start, rows), :]


def merged(parts):
    peak = functools.reduce(jnp.maximum, [p[0] for p in parts])
    scaled = [jnp.stack([p[1] * jnp.exp(p[0] - peak), p[2]]) for p in parts]
    return jnp.stack([peak, *total(scaled)])


def total(parts):
    if len(parts) == 2:
        return parts[0] + parts[1]
    return (parts[0] + parts[2]) + (parts[1] + parts[3])


def shards(hidden, head_weight, labels, loss_mask):
    weights = head_weight[0]
    words, feats = weights.shape
    place = jnp.stack([lax.axis_index(a) for a in ("y", "x", "core", "tok")]).astype(jnp.int32)
    is_teacher = lax.axis_index("grp") == 0
    first_word = lax.axis_index(("y", "x", "core", "tok")) * words
    word_ids = first_word + lax.broadcasted_iota(jnp.int32, (words, 1), 0)
    mask = loss_mask.astype(F32)

    block = hidden[0]
    piece = jax.ShapeDtypeStruct(block.shape, block.dtype)
    by_tok = kernel_call(
        order_tok_kernel,
        [piece] * 4,
        place,
        *gathered(block, "tok"),
        scratch=[pltpu.VMEM((4,) + block.shape, block.dtype)],
    )
    rows = block.shape[0]
    chunk = 2 * rows

    def scores(c):
        u = jnp.stack(gathered(by_tok[2 * c], "x"))
        v = jnp.stack(gathered(by_tok[2 * c + 1], "y"))
        us = gathered(u, "y")
        vs = gathered(v, "x")
        other = shifts(jnp.stack(us + vs), "core", 1)
        joined = kernel_call(
            join_features_kernel,
            jax.ShapeDtypeStruct((chunk, feats), block.dtype),
            place,
            *us,
            *vs,
            other,
        )
        z = lax.dot_general(
            weights, joined, (((1,), (1,)), ((), ())), preferred_element_type=F32
        ).astype(BF16)
        return lax.optimization_barrier(z)

    def norms(z, hit):
        z = z.astype(F32)
        peak = jnp.max(z, axis=0)
        stats = jnp.stack(
            [
                peak,
                jnp.sum(jnp.exp(z - peak), axis=0),
                jnp.sum(jnp.where(hit, z, 0.0), axis=0),
            ]
        )
        for axis in ("core", "x", "y", "tok"):
            stats = merged(gathered(stats, axis))
        return stats[0] + jnp.log(stats[1]), stats[2]

    def reduced(partial, c):
        keep_x, keep_y, send_x, send_y = split_features(place, partial)
        got_x = student_shifts(send_x, "core", 1)
        got_y = student_shifts(send_y, "core", 1)
        xs = [keep_x[k] + got_x[k] for k in range(4)]
        ys = [keep_y[k] + got_y[k] for k in range(4)]
        xs = [xs[0]] + [student_shifts(xs[k], "x", k) for k in range(1, 4)]
        ys = [ys[0]] + [student_shifts(ys[k], "y", k) for k in range(1, 4)]
        xs = total(xs)
        ys = total(ys)
        xs = [xs[0]] + [student_shifts(xs[k], "y", k) for k in range(1, 4)]
        ys = [ys[0]] + [student_shifts(ys[k], "x", k) for k in range(1, 4)]
        part = jax.ShapeDtypeStruct((chunk // 4, xs[0].shape[1]), F32)
        ends = kernel_call(
            split_rows_kernel,
            [part] * 4,
            place,
            *xs,
            *ys,
            scratch=[pltpu.VMEM((chunk, xs[0].shape[1]), F32)],
        )
        ends = [ends[0]] + [student_shifts(ends[k], "tok", k) for k in range(1, 4)]
        return total(ends).astype(BF16)

    zs, hits, sent, normed = [], [], [], []
    for c in range(2):
        span = slice(c * chunk, (c + 1) * chunk)
        zs.append(scores(c))
        hits.append(word_ids == labels[span][None, :])
        sent.append(lax.ppermute(zs[c], "grp", [(0, 1)]))
    blocks, diverge = [], []
    student_norms, teacher_norms, label_logits = [], [], []
    for c in range(2):
        span = slice(c * chunk, (c + 1) * chunk)
        norm, label_logit = norms(zs[c], hits[c])
        teacher_norm = lax.ppermute(norm, "grp", [(0, 1)])
        student_norms.append(norm)
        teacher_norms.append(teacher_norm)
        label_logits.append(label_logit)
        teacher_logp = sent[c].astype(F32) - teacher_norm
        student_logp = zs[c].astype(F32) - norm
        teacher_prob = jnp.exp(teacher_logp)
        student_prob = jnp.exp(student_logp)
        diverge.append(jnp.sum(teacher_prob * (teacher_logp - student_logp), axis=0))
        grads = (
            (2.0 * student_prob - teacher_prob - hits[c].astype(F32)) * mask[span]
        ).astype(BF16)
        partial = lax.dot_general(
            grads, weights, (((0,), (0,)), ((), ())), preferred_element_type=F32
        )
        blocks.append(reduced(partial, c))
    diverged = jnp.concatenate(diverge).reshape(8, -1)
    for axis in ("core", "x", "y", "tok"):
        diverged = total(
            [diverged]
            + [student_shifts(diverged, axis, k) for k in range(1, lax.axis_size(axis))]
        )
    teacher_norm = jnp.concatenate(teacher_norms)
    student_norm = jnp.concatenate(student_norms)
    token_loss = mask * (
        diverged.reshape(-1) + student_norm - jnp.concatenate(label_logits)
    )
    small = jnp.stack([token_loss, teacher_norm, student_norm])
    handed = lax.ppermute(small, "grp", [(1, 0)])
    small = jnp.where(is_teacher, handed, small)
    handed_rows = lax.ppermute(blocks[0], "grp", [(1, 0)])
    input_grads = jnp.where(is_teacher, handed_rows, blocks[1])
    return (input_grads, small[0], small[1:])


def solution(mesh):
    fine = Mesh(mesh.devices.reshape(2, 4, 4, 2, 4), ("grp", "y", "x", "core", "tok"))
    vocab = ("y", "x", "core")
    return jax.shard_map(
        shards,
        mesh=fine,
        in_specs=(
            P("grp", "tok", vocab),
            P("grp", vocab + ("tok",), None),
            P(),
            P(),
        ),
        out_specs=(P(("grp", "tok"), vocab), P(), P()),
        check_vma=False,
    )
```

```python
import functools
import jax
import jax.numpy as jnp
from jax import lax
from jax.experimental import pallas as pl
from jax.experimental.pallas import tpu as pltpu
from jax.sharding import Mesh, PartitionSpec as P

BF16 = jnp.bfloat16
F32 = jnp.float32
VMEM_LIMIT = 50 * 1024 * 1024
EXTRA = 8


def shifts(x, axis, step):
    size = lax.axis_size(axis)
    return lax.ppermute(x, axis, [(i, (i + step) % size) for i in range(size)])


def student_shifts(x, axis, step):
    size = lax.axis_size(axis)
    return lax.ppermute(
        x, ("grp", axis), [(size + i, size + (i + step) % size) for i in range(size)]
    )


def gathered(x, axis):
    return [x] + [shifts(x, axis, k) for k in range(1, lax.axis_size(axis))]


def scattered(parts, axis):
    return [parts[0]] + [student_shifts(parts[k], axis, k) for k in range(1, len(parts))]


def in_vmem():
    return pl.BlockSpec(memory_space=pltpu.VMEM)


def vmem_call(kernel, out_shape, *arrays, place=None, scratch=()):
    scalars = [] if place is None else [place]
    return pl.pallas_call(
        kernel,
        out_shape=out_shape,
        in_specs=[pl.BlockSpec(memory_space=pltpu.SMEM)] * len(scalars)
        + [in_vmem()] * len(arrays),
        out_specs=jax.tree.map(lambda _: in_vmem(), out_shape),
        scratch_shapes=list(scratch),
        compiler_params=pltpu.CompilerParams(vmem_limit_bytes=VMEM_LIMIT),
    )(*scalars, *arrays)


def order_tok_kernel(place_ref, p0, p1, p2, p3, lower, upper, held):
    me = place_ref[3]
    rows = p0.shape[0]
    for k, piece in enumerate((p0, p1, p2, p3)):
        held[lax.rem(me + 4 - k, 4)] = piece[...]
    lower[:rows] = held[0]
    lower[rows:] = held[1]
    upper[:rows] = held[2]
    upper[rows:] = held[3]


def stack_kernel(u0, u1, u2, u3, v0, v1, v2, v3, u_out, v_out):
    for k, piece in enumerate((u0, u1, u2, u3)):
        u_out[k] = piece[...]
    for k, piece in enumerate((v0, v1, v2, v3)):
        v_out[k] = piece[...]


def order_chips_kernel(place_ref, u0, u1, u2, u3, v0, v1, v2, v3, out):
    y, x = place_ref[0], place_ref[1]
    rows, wide = u0.shape[1:]
    for ky in range(4):
        for kx in range(4):
            chip = lax.rem(y + 4 - ky, 4) * 4 + lax.rem(x + 4 - kx, 4)
            out[chip, :rows] = (u0, u1, u2, u3)[ky][kx]
            out[chip, rows:] = (v0, v1, v2, v3)[kx][ky]


def join_cores_kernel(place_ref, own, sibling, lower, upper):
    core = place_ref[2]
    chips, rows, wide = own.shape
    half = rows // 2
    for chip in range(chips):
        first = jnp.where(core == 0, own[chip], sibling[chip])
        second = jnp.where(core == 0, sibling[chip], own[chip])
        at = 2 * chip * wide
        lower[:, at : at + wide] = first[:half]
        lower[:, at + wide : at + 2 * wide] = second[:half]
        upper[:, at : at + wide] = first[half:]
        upper[:, at + wide : at + 2 * wide] = second[half:]


def merge_kernel(*refs):
    parts, out = refs[:-1], refs[-1]
    peak = functools.reduce(jnp.maximum, [p[0:1] for p in parts])
    out[0:1] = peak
    out[1:2] = total([p[1:2] * jnp.exp(p[0:1] - peak) for p in parts])
    out[2:3] = total([p[2:3] for p in parts])


def total(parts):
    if len(parts) == 2:
        return parts[0] + parts[1]
    return (parts[0] + parts[2]) + (parts[1] + parts[3])


def grads_kernel(place_ref, grads, weights, extra, keep, send, turned):
    step = pl.program_id(0)
    core = place_ref[2]

    @pl.when(step == 0)
    def _():
        turned[...] = grads[...].T

    tokens = grads.shape[1]
    wide = weights.shape[1] // 2
    full = jnp.dot(turned[...], weights[...], preferred_element_type=F32)
    low = full[:, :wide]
    high = full[:, wide:]
    first = step // 4
    second = step % 4
    at = pl.ds(pl.multiple_of(second * tokens, tokens), tokens)
    keep[first, at] = jnp.where(core == 0, low, high)
    send[first, at] = jnp.where(core == 0, high, low)

    @pl.when(second == 0)
    def _():
        keep[first, 4 * tokens :] = extra[...]
        send[first, 4 * tokens :] = extra[...]


def split_grads(place, grads, weights, extra, x_first):
    words, tokens = grads.shape
    wide = weights.shape[1] // 16

    def chip(i, p):
        kx, ky = (i // 4, i % 4) if x_first else (i % 4, i // 4)
        return (0, lax.rem(p[0] + ky, 4) * 4 + lax.rem(p[1] + kx, 4))

    part = jax.ShapeDtypeStruct((4, 4 * tokens + EXTRA, wide // 2), F32)
    return pl.pallas_call(
        grads_kernel,
        out_shape=[part] * 2,
        grid_spec=pltpu.PrefetchScalarGridSpec(
            num_scalar_prefetch=1,
            grid=(16,),
            in_specs=[in_vmem(), pl.BlockSpec((words, wide), chip), in_vmem()],
            out_specs=[in_vmem()] * 2,
            scratch_shapes=[pltpu.VMEM((tokens, words), BF16)],
        ),
        compiler_params=pltpu.CompilerParams(vmem_limit_bytes=VMEM_LIMIT),
    )(place, grads, weights, extra)


def pair_sum_kernel(keep, got, *outs):
    for k, out in enumerate(outs):
        out[...] = keep[k] + got[k]


def line_sum_kernel(p0, p1, p2, p3, *outs):
    rows = outs[0].shape[0] - EXTRA
    tail = pl.ds(4 * rows, EXTRA)
    extra = total([p0[tail], p1[tail], p2[tail], p3[tail]])
    for k, out in enumerate(outs):
        at = pl.ds(k * rows, rows)
        out[:rows] = total([p0[at], p1[at], p2[at], p3[at]])
        out[rows:] = extra


def last_split_kernel(place_ref, a0, a1, a2, a3, b0, b1, b2, b3, *refs):
    outs, held = refs[:8], refs[8]
    me = place_ref[3]
    rows = a0.shape[0] - EXTRA
    held[0] = total([a0[...], a1[...], a2[...], a3[...]])
    held[1] = total([b0[...], b1[...], b2[...], b3[...]])
    part = rows // 4
    for k in range(4):
        start = pl.multiple_of(lax.rem(me + k, 4) * part, part)
        for half in range(2):
            out = outs[4 * half + k]
            out[:part] = held[half, pl.ds(start, part)]
            out[part : part + EXTRA] = held[0, rows:]
            out[part + EXTRA :] = held[1, rows:]


def shards(hidden, head_weight, labels, loss_mask):
    weights = head_weight[0]
    words, feats = weights.shape
    place = jnp.stack([lax.axis_index(a) for a in ("y", "x", "core", "tok")]).astype(jnp.int32)
    is_teacher = lax.axis_index("grp") == 0
    first_word = lax.axis_index(("y", "x", "core", "tok")) * words
    word_ids = first_word + lax.broadcasted_iota(jnp.int32, (words, 1), 0)
    mask = loss_mask.astype(F32)

    block = hidden[0]
    rows, wide = block.shape
    half = 2 * rows
    array = jax.ShapeDtypeStruct
    lower, upper = vmem_call(
        order_tok_kernel,
        [array((half, wide), BF16)] * 2,
        *gathered(block, "tok"),
        place=place,
        scratch=[pltpu.VMEM((4, rows, wide), BF16)],
    )
    u, v = vmem_call(
        stack_kernel,
        [array((4, half, wide), BF16)] * 2,
        *gathered(lower, "x"),
        *gathered(upper, "y"),
    )
    own = vmem_call(
        order_chips_kernel,
        array((16, 2 * half, wide), BF16),
        *gathered(u, "y"),
        *gathered(v, "x"),
        place=place,
    )
    inputs = vmem_call(
        join_cores_kernel,
        [array((half, feats), BF16)] * 2,
        own,
        shifts(own, "core", 1),
        place=place,
    )

    own_z, sent = [], []
    for c in range(2):
        z = lax.dot_general(
            weights, inputs[c], (((1,), (1,)), ((), ())), preferred_element_type=F32
        ).astype(BF16)
        own_z.append(lax.optimization_barrier(z))
        sent.append(lax.ppermute(own_z[c], "grp", [(0, 1)]))

    hits = [word_ids == labels[c * half : (c + 1) * half][None, :] for c in range(2)]
    stats = []
    for c in range(2):
        z = own_z[c].astype(F32)
        peak = jnp.max(z, axis=0)
        stats.append(
            jnp.stack(
                [
                    peak,
                    jnp.sum(jnp.exp(z - peak), axis=0),
                    jnp.sum(jnp.where(hits[c], z, 0.0), axis=0),
                ]
            )
        )
    stats = jnp.concatenate(stats, axis=1)
    for axis in ("core", "x", "y", "tok"):
        stats = vmem_call(merge_kernel, array(stats.shape, F32), *gathered(stats, axis))
    own_norm = stats[0] + jnp.log(stats[1])
    told = jnp.stack([own_norm, stats[2]])
    heard = lax.ppermute(told, "grp", [(0, 1), (1, 0)])
    teacher_norm = jnp.where(is_teacher, own_norm, heard[0])
    student_norm = jnp.where(is_teacher, heard[0], own_norm)
    label_logit = jnp.where(is_teacher, heard[1], stats[2])

    ends = []
    for c in range(2):
        span = slice(c * half, (c + 1) * half)
        teacher_logp = sent[c].astype(F32) - teacher_norm[span]
        student_logp = own_z[c].astype(F32) - student_norm[span]
        teacher_prob = jnp.exp(teacher_logp)
        student_prob = jnp.exp(student_logp)
        diverge = jnp.sum(teacher_prob * (teacher_logp - student_logp), axis=0)
        grads = (
            (2.0 * student_prob - teacher_prob - hits[c].astype(F32)) * mask[span]
        ).astype(BF16)
        extra = jnp.zeros((EXTRA, wide), F32).at[:2].set(diverge.reshape(2, wide))
        keep, send = split_grads(place, grads, weights, extra, c == 0)
        axes = ("x", "y") if c == 0 else ("y", "x")
        parts = vmem_call(
            pair_sum_kernel,
            [array(keep.shape[1:], F32)] * 4,
            keep,
            student_shifts(send, "core", 1),
        )
        parts = vmem_call(
            line_sum_kernel,
            [array((half + EXTRA, wide), F32)] * 4,
            *scattered(parts, axes[0]),
        )
        ends += scattered(parts, axes[1])

    part = half // 4
    last = vmem_call(
        last_split_kernel,
        [array((part + 2 * EXTRA, wide), F32)] * 8,
        *ends,
        place=place,
        scratch=[pltpu.VMEM((2, half + EXTRA, wide), F32)],
    )
    for_teacher, for_student = last[:4], last[4:]
    got_student = scattered(for_student, "tok")
    got_teacher = [
        lax.ppermute(
            for_teacher[k], ("grp", "tok"), [(4 + i, (i + k) % 4) for i in range(4)]
        )
        for k in range(4)
    ]
    mine = total([jnp.where(is_teacher, t, s) for t, s in zip(got_teacher, got_student)])
    input_grads = mine[:part].astype(BF16)
    diverged = jnp.concatenate([mine[part : part + 2], mine[part + EXTRA : part + EXTRA + 2]])
    token_loss = mask * (diverged.reshape(-1) + student_norm - label_logit)
    return (input_grads, token_loss, jnp.stack([teacher_norm, student_norm]))


def solution(mesh):
    fine = Mesh(mesh.devices.reshape(2, 4, 4, 2, 4), ("grp", "y", "x", "core", "tok"))
    vocab = ("y", "x", "core")
    return jax.shard_map(
        shards,
        mesh=fine,
        in_specs=(
            P("grp", "tok", vocab),
            P("grp", vocab + ("tok",), None),
            P(),
            P(),
        ),
        out_specs=(P(("grp", "tok"), vocab), P(), P()),
        check_vma=False,
    )
```

```python
import functools
import jax
import jax.numpy as jnp
from jax import lax
from jax.experimental import pallas as pl
from jax.experimental.pallas import tpu as pltpu
from jax.sharding import Mesh, PartitionSpec as P

BF16 = jnp.bfloat16
F32 = jnp.float32
VMEM_LIMIT = 50 * 1024 * 1024
EXTRA = 8


def shifts(x, axis, step):
    size = lax.axis_size(axis)
    return lax.ppermute(x, axis, [(i, (i + step) % size) for i in range(size)])


def student_shifts(x, axis, step):
    size = lax.axis_size(axis)
    return lax.ppermute(
        x, ("grp", axis), [(size + i, size + (i + step) % size) for i in range(size)]
    )


def gathered(x, axis):
    return [x] + [shifts(x, axis, k) for k in range(1, lax.axis_size(axis))]


def scattered(parts, axis):
    return [parts[0]] + [student_shifts(parts[k], axis, k) for k in range(1, len(parts))]


def in_vmem():
    return pl.BlockSpec(memory_space=pltpu.VMEM)


def vmem_call(kernel, out_shape, *arrays, place=None, scratch=()):
    scalars = [] if place is None else [place]
    return pl.pallas_call(
        kernel,
        out_shape=out_shape,
        in_specs=[pl.BlockSpec(memory_space=pltpu.SMEM)] * len(scalars)
        + [in_vmem()] * len(arrays),
        out_specs=jax.tree.map(lambda _: in_vmem(), out_shape),
        scratch_shapes=list(scratch),
        compiler_params=pltpu.CompilerParams(vmem_limit_bytes=VMEM_LIMIT),
    )(*scalars, *arrays)


def order_tok_kernel(place_ref, p0, p1, p2, p3, lower, upper, held):
    me = place_ref[3]
    rows = p0.shape[0]
    for k, piece in enumerate((p0, p1, p2, p3)):
        held[lax.rem(me + 4 - k, 4)] = piece[...]
    lower[:rows] = held[0]
    lower[rows:] = held[1]
    upper[:rows] = held[2]
    upper[rows:] = held[3]


def stack_kernel(u0, u1, u2, u3, v0, v1, v2, v3, u_out, v_out):
    for k, piece in enumerate((u0, u1, u2, u3)):
        u_out[k] = piece[...]
    for k, piece in enumerate((v0, v1, v2, v3)):
        v_out[k] = piece[...]


def order_chips_kernel(place_ref, u0, u1, u2, u3, v0, v1, v2, v3, out):
    y, x = place_ref[0], place_ref[1]
    rows, wide = u0.shape[1:]
    for ky in range(4):
        for kx in range(4):
            chip = lax.rem(y + 4 - ky, 4) * 4 + lax.rem(x + 4 - kx, 4)
            out[chip, :rows] = (u0, u1, u2, u3)[ky][kx]
            out[chip, rows:] = (v0, v1, v2, v3)[kx][ky]


def scores_kernel(place_ref, weights, own, sibling, lower, upper, joined, held, acc, sems):
    core = place_ref[2]
    chips, _, wide = own.shape
    strips, words, depth = held.shape
    half = lower.shape[1]
    copies = [
        pltpu.make_async_copy(weights.at[:, pl.ds(i * depth, depth)], held.at[i], sems.at[i])
        for i in range(strips)
    ]
    for copy in copies:
        copy.start()

    def join(first, second):
        for chip in range(chips):
            at = 2 * chip * wide
            joined[:, at : at + wide] = first[chip]
            joined[:, at + wide : at + 2 * wide] = second[chip]

    @pl.when(core == 0)
    def _():
        join(own, sibling)

    @pl.when(core != 0)
    def _():
        join(sibling, own)

    tall = 608
    for i in range(strips):
        copies[i].wait()
        for start in range(0, words, tall):
            at = slice(start, min(start + tall, words))
            part = lax.dot_general(
                held[i, at],
                joined[:, i * depth : (i + 1) * depth],
                (((1,), (1,)), ((), ())),
                preferred_element_type=F32,
            )
            if i > 0:
                part = acc[at] + part
            if i < strips - 1:
                acc[at] = part
            else:
                lower[at] = part[:, :half].astype(BF16)
                upper[at] = part[:, half:].astype(BF16)


def scores(place, weights, own, sibling):
    words, feats = weights.shape
    tokens = own.shape[1]
    strips = 4
    part = jax.ShapeDtypeStruct((words, tokens // 2), BF16)
    return pl.pallas_call(
        scores_kernel,
        out_shape=[part] * 2,
        in_specs=[
            pl.BlockSpec(memory_space=pltpu.SMEM),
            pl.BlockSpec(memory_space=pl.ANY),
            in_vmem(),
            in_vmem(),
        ],
        out_specs=[in_vmem()] * 2,
        scratch_shapes=[
            pltpu.VMEM((tokens, feats), BF16),
            pltpu.VMEM((strips, words, feats // strips), BF16),
            pltpu.VMEM((words, tokens), F32),
            pltpu.SemaphoreType.DMA((strips,)),
        ],
        compiler_params=pltpu.CompilerParams(vmem_limit_bytes=VMEM_LIMIT),
    )(place, weights, own, sibling)


def merge_kernel(*refs):
    parts, out = refs[:-1], refs[-1]
    peak = functools.reduce(jnp.maximum, [p[0:1] for p in parts])
    out[0:1] = peak
    out[1:2] = total([p[1:2] * jnp.exp(p[0:1] - peak) for p in parts])
    out[2:3] = total([p[2:3] for p in parts])


def norms_kernel(place_ref, *refs):
    parts, out, held = refs[:8], refs[8], refs[9]
    me = place_ref[4]
    for k, piece in enumerate(parts):
        held[lax.rem(me + 8 - k, 8)] = piece[...]
    for group in range(2):
        planes = [held[4 * group + i] for i in range(4)]
        peak = functools.reduce(jnp.maximum, [p[0:1] for p in planes])
        out[group : group + 1] = peak + jnp.log(
            total([p[1:2] * jnp.exp(p[0:1] - peak) for p in planes])
        )
    out[2:3] = total([held[4 + i, 2:3] for i in range(4)])


def total(parts):
    if len(parts) == 2:
        return parts[0] + parts[1]
    return (parts[0] + parts[2]) + (parts[1] + parts[3])


def grads_kernel(x_first, place_ref, grads, weights, extra, keep, send, turned):
    y, x, core = place_ref[0], place_ref[1], place_ref[2]
    tokens = grads.shape[1]
    wide = keep.shape[2]
    turned[...] = grads[...].T
    for first in range(4):
        for second in range(4):
            kx, ky = (first, second) if x_first else (second, first)
            chip = lax.rem(y + ky, 4) * 4 + lax.rem(x + kx, 4)
            columns = pl.ds(pl.multiple_of(chip * 2 * wide, 2 * wide), 2 * wide)
            full = jnp.dot(turned[...], weights[:, columns], preferred_element_type=F32)
            low = full[:, :wide]
            high = full[:, wide:]
            at = slice(second * tokens, (second + 1) * tokens)
            keep[first, at] = jnp.where(core == 0, low, high)
            send[first, at] = jnp.where(core == 0, high, low)
        keep[first, 4 * tokens :] = extra[...]
        send[first, 4 * tokens :] = extra[...]


def split_grads(place, grads, weights, extra, x_first):
    words, tokens = grads.shape
    wide = weights.shape[1] // 32
    part = jax.ShapeDtypeStruct((4, 4 * tokens + EXTRA, wide), F32)
    return vmem_call(
        functools.partial(grads_kernel, x_first),
        [part] * 2,
        grads,
        weights,
        extra,
        place=place,
        scratch=[pltpu.VMEM((tokens, words), BF16)],
    )


def pair_sum_kernel(keep, got, *outs):
    for k, out in enumerate(outs):
        out[...] = keep[k] + got[k]


def line_sum_kernel(p0, p1, p2, p3, *outs):
    rows = outs[0].shape[0] - EXTRA
    tail = pl.ds(4 * rows, EXTRA)
    extra = total([p0[tail], p1[tail], p2[tail], p3[tail]])
    for k, out in enumerate(outs):
        at = pl.ds(k * rows, rows)
        out[:rows] = total([p0[at], p1[at], p2[at], p3[at]])
        out[rows:] = extra


def last_split_kernel(place_ref, a0, a1, a2, a3, b0, b1, b2, b3, *refs):
    outs, held = refs[:8], refs[8]
    me = place_ref[3]
    rows = a0.shape[0] - EXTRA
    held[0] = total([a0[...], a1[...], a2[...], a3[...]])
    held[1] = total([b0[...], b1[...], b2[...], b3[...]])
    part = rows // 4
    for k in range(4):
        start = pl.multiple_of(lax.rem(me + k, 4) * part, part)
        for half in range(2):
            out = outs[4 * half + k]
            out[:part] = held[half, pl.ds(start, part)]
            out[part : part + EXTRA] = held[0, rows:]
            out[part + EXTRA :] = held[1, rows:]


def shards(hidden, head_weight, labels, loss_mask):
    weights = head_weight[0]
    words, feats = weights.shape
    axes = ("y", "x", "core", "tok", ("grp", "tok"))
    place = jnp.stack([lax.axis_index(a) for a in axes]).astype(jnp.int32)
    is_teacher = lax.axis_index("grp") == 0
    first_word = lax.axis_index(("y", "x", "core", "tok")) * words
    word_ids = first_word + lax.broadcasted_iota(jnp.int32, (words, 1), 0)
    mask = loss_mask.astype(F32)

    block = hidden[0]
    rows, wide = block.shape
    half = 2 * rows
    array = jax.ShapeDtypeStruct
    lower, upper = vmem_call(
        order_tok_kernel,
        [array((half, wide), BF16)] * 2,
        *gathered(block, "tok"),
        place=place,
        scratch=[pltpu.VMEM((4, rows, wide), BF16)],
    )
    u, v = vmem_call(
        stack_kernel,
        [array((4, half, wide), BF16)] * 2,
        *gathered(lower, "x"),
        *gathered(upper, "y"),
    )
    own = vmem_call(
        order_chips_kernel,
        array((16, 2 * half, wide), BF16),
        *gathered(u, "y"),
        *gathered(v, "x"),
        place=place,
    )
    own_z = scores(place, weights, own, shifts(own, "core", 1))
    mirrored = [
        lax.ppermute(z, ("grp", "tok"), [(i, 7 - i) for i in range(4)]) for z in own_z
    ]

    hits = [word_ids == labels[c * half : (c + 1) * half][None, :] for c in range(2)]
    stats = []
    for c in range(2):
        z = own_z[c].astype(F32)
        peak = jnp.max(z, axis=0)
        stats.append(
            jnp.stack(
                [
                    peak,
                    jnp.sum(jnp.exp(z - peak), axis=0),
                    jnp.sum(jnp.where(hits[c], z, 0.0), axis=0),
                ]
            )
        )
    stats = jnp.concatenate(stats, axis=1)
    for axis in ("core", "x", "y"):
        stats = vmem_call(merge_kernel, array(stats.shape, F32), *gathered(stats, axis))
    mirrored[0], stats = lax.optimization_barrier((mirrored[0], stats))
    sent = [
        lax.ppermute(z, ("grp", "tok"), [(4 + i, 7 - i) for i in range(4)])
        for z in mirrored
    ]
    teacher_norm, student_norm, label_logit = vmem_call(
        norms_kernel,
        array(stats.shape, F32),
        *gathered(stats, ("grp", "tok")),
        place=place,
        scratch=[pltpu.VMEM((8,) + stats.shape, F32)],
    )

    ends = []
    for c in range(2):
        span = slice(c * half, (c + 1) * half)
        teacher_logp = sent[c].astype(F32) - teacher_norm[span]
        student_logp = own_z[c].astype(F32) - student_norm[span]
        teacher_prob = jnp.exp(teacher_logp)
        student_prob = jnp.exp(student_logp)
        diverge = jnp.sum(teacher_prob * (teacher_logp - student_logp), axis=0)
        grads = (
            (2.0 * student_prob - teacher_prob - hits[c].astype(F32)) * mask[span]
        ).astype(BF16)
        extra = jnp.zeros((EXTRA, wide), F32).at[:2].set(diverge.reshape(2, wide))
        keep, send = split_grads(place, grads, weights, extra, c == 0)
        axes = ("x", "y") if c == 0 else ("y", "x")
        parts = vmem_call(
            pair_sum_kernel,
            [array(keep.shape[1:], F32)] * 4,
            keep,
            student_shifts(send, "core", 1),
        )
        parts = vmem_call(
            line_sum_kernel,
            [array((half + EXTRA, wide), F32)] * 4,
            *scattered(parts, axes[0]),
        )
        ends += scattered(parts, axes[1])

    part = half // 4
    last = vmem_call(
        last_split_kernel,
        [array((part + 2 * EXTRA, wide), F32)] * 8,
        *ends,
        place=place,
        scratch=[pltpu.VMEM((2, half + EXTRA, wide), F32)],
    )
    for_teacher, for_student = last[:4], last[4:]
    got_student = scattered(for_student, "tok")
    got_teacher = [
        lax.ppermute(
            for_teacher[k], ("grp", "tok"), [(4 + i, (i + k) % 4) for i in range(4)]
        )
        for k in range(4)
    ]
    mine = total([jnp.where(is_teacher, t, s) for t, s in zip(got_teacher, got_student)])
    input_grads = mine[:part].astype(BF16)
    diverged = jnp.concatenate([mine[part : part + 2], mine[part + EXTRA : part + EXTRA + 2]])
    token_loss = mask * (diverged.reshape(-1) + student_norm - label_logit)
    return (input_grads, token_loss, jnp.stack([teacher_norm, student_norm]))


def solution(mesh):
    fine = Mesh(mesh.devices.reshape(2, 4, 4, 2, 4), ("grp", "y", "x", "core", "tok"))
    vocab = ("y", "x", "core")
    return jax.shard_map(
        shards,
        mesh=fine,
        in_specs=(
            P("grp", "tok", vocab),
            P("grp", vocab + ("tok",), None),
            P(),
            P(),
        ),
        out_specs=(P(("grp", "tok"), vocab), P(), P()),
        check_vma=False,
    )
```

```python
import functools
import jax
import jax.numpy as jnp
from jax import lax
from jax.experimental import pallas as pl
from jax.experimental.pallas import tpu as pltpu
from jax.sharding import Mesh, PartitionSpec as P

BF16 = jnp.bfloat16
F32 = jnp.float32
VMEM_LIMIT = 50 * 1024 * 1024
EXTRA = 8
STRIPS = 4
CHIPS = ("y", "x")
PLANES = ("grp", "tok")


def in_vmem():
    return pl.BlockSpec(memory_space=pltpu.VMEM)


def in_smem():
    return pl.BlockSpec(memory_space=pltpu.SMEM)


def vmem_call(kernel, out_shape, *arrays, place=None, weights=None, scratch=()):
    scalars = [] if place is None else [place]
    remote = [] if weights is None else [weights]
    return pl.pallas_call(
        kernel,
        out_shape=out_shape,
        in_specs=[in_smem()] * len(scalars)
        + [pl.BlockSpec(memory_space=pl.ANY)] * len(remote)
        + [in_vmem()] * len(arrays),
        out_specs=jax.tree.map(lambda _: in_vmem(), out_shape),
        scratch_shapes=list(scratch),
        compiler_params=pltpu.CompilerParams(vmem_limit_bytes=VMEM_LIMIT),
    )(*scalars, *remote, *arrays)


def swapped(x, axis):
    return lax.ppermute(x, axis, [(0, 1), (1, 0)])


def swapped_in_student(x):
    return lax.ppermute(x, ("grp", "core"), [(2, 3), (3, 2)])


def exchanged(x, axes):
    return lax.all_to_all(x, axes, 0, 0)


def order_tok_kernel(place_ref, p0, p1, p2, p3, lower, upper, held):
    me = place_ref[1]
    rows = p0.shape[0]
    for k, piece in enumerate((p0, p1, p2, p3)):
        held[lax.rem(me + 4 - k, 4)] = piece[...]
    for chip in range(lower.shape[0]):
        lower[chip, :rows] = held[0]
        lower[chip, rows:] = held[1]
        upper[chip, :rows] = held[2]
        upper[chip, rows:] = held[3]


def strips_of(weights, held, sems):
    depth = held.shape[2]
    copies = [
        pltpu.make_async_copy(weights.at[:, pl.ds(i * depth, depth)], held.at[i], sems.at[i])
        for i in range(STRIPS)
    ]
    for copy in copies:
        copy.start()
    return copies


def scores_kernel(place_ref, weights, own, sibling, out, joined, held, acc, sems):
    core = place_ref[0]
    chips, _, wide = own.shape
    depth = held.shape[2]
    words = out.shape[0]
    copies = strips_of(weights, held, sems)

    def join(first, second):
        for chip in range(chips):
            at = 2 * chip * wide
            joined[:, at : at + wide] = first[chip]
            joined[:, at + wide : at + 2 * wide] = second[chip]

    @pl.when(core == 0)
    def _():
        join(own, sibling)

    @pl.when(core != 0)
    def _():
        join(sibling, own)

    tall = 608
    for i in range(STRIPS):
        copies[i].wait()
        for start in range(0, words, tall):
            at = slice(start, min(start + tall, words))
            part = lax.dot_general(
                held[i, at],
                joined[:, i * depth : (i + 1) * depth],
                (((1,), (1,)), ((), ())),
                preferred_element_type=F32,
            )
            if i > 0:
                part = acc[at] + part
            if i < STRIPS - 1:
                acc[at] = part
            else:
                out[at] = part.astype(BF16)


def scores(place, weights, own):
    words, feats = weights.shape
    tokens = own.shape[1]
    return vmem_call(
        scores_kernel,
        jax.ShapeDtypeStruct((words, tokens), BF16),
        own,
        swapped(own, "core"),
        place=place,
        weights=weights,
        scratch=[
            pltpu.VMEM((tokens, feats), BF16),
            pltpu.VMEM((STRIPS, words, feats // STRIPS), BF16),
            pltpu.VMEM((words, tokens), F32),
            pltpu.SemaphoreType.DMA((STRIPS,)),
        ],
    )


def total(parts):
    parts = list(parts)
    while len(parts) > 1:
        parts = [a + b for a, b in zip(parts[::2], parts[1::2])]
    return parts[0]


def merge(parts):
    peak = functools.reduce(jnp.maximum, [p[0:1] for p in parts])
    mass = total([p[1:2] * jnp.exp(p[0:1] - peak) for p in parts])
    return peak, mass, total([p[2:3] for p in parts])


def pair_kernel(mine, other, out):
    merged = merge([mine[...], other[...]])
    for copy in range(out.shape[0]):
        for row in range(3):
            out[copy, row : row + 1] = merged[row]


def chips_kernel(parts, out):
    merged = merge([parts[i] for i in range(parts.shape[0])])
    for copy in range(out.shape[0]):
        for row in range(3):
            out[copy, row : row + 1] = merged[row]


def planes_kernel(parts, out):
    for group in range(2):
        peak, mass, label = merge([parts[4 * group + i] for i in range(4)])
        out[group : group + 1] = peak + jnp.log(mass)
    out[2:3] = label


def grads_kernel(place_ref, weights, grads, extra, keep, send, turned, held, sems):
    core = place_ref[0]
    tokens = grads.shape[1]
    chips, _, wide = keep.shape
    copies = strips_of(weights, held, sems)
    turned[...] = grads[...].T
    per_strip = chips // STRIPS
    for chip in range(chips):
        strip, at = chip // per_strip, (chip % per_strip) * 2 * wide
        if at == 0:
            copies[strip].wait()
        full = jnp.dot(
            turned[...], held[strip, :, at : at + 2 * wide], preferred_element_type=F32
        )
        low = full[:, :wide]
        high = full[:, wide:]
        keep[chip, :tokens] = jnp.where(core == 0, low, high)
        send[chip, :tokens] = jnp.where(core == 0, high, low)
        keep[chip, tokens:] = extra[...]
        send[chip, tokens:] = extra[...]


def split_grads(place, weights, grads, extra):
    words, tokens = grads.shape
    feats = weights.shape[1]
    wide = extra.shape[1]
    part = jax.ShapeDtypeStruct((feats // (2 * wide), tokens + EXTRA, wide), F32)
    return vmem_call(
        grads_kernel,
        [part] * 2,
        grads,
        extra,
        place=place,
        weights=weights,
        scratch=[
            pltpu.VMEM((tokens, words), BF16),
            pltpu.VMEM((STRIPS, words, feats // STRIPS), BF16),
            pltpu.SemaphoreType.DMA((STRIPS,)),
        ],
    )


def pair_sum_kernel(keep, got, out):
    out[...] = keep[...] + got[...]


def last_split_kernel(lower, upper, out):
    rows = lower.shape[1] - EXTRA
    part = rows // 4
    chips = lower.shape[0]
    tail = [total([half[i, rows:] for i in range(chips)]) for half in (lower, upper)]
    for plane in range(8):
        half = lower if plane < 4 else upper
        at = slice((plane % 4) * part, (plane % 4 + 1) * part)
        out[plane, :part] = total([half[i, at] for i in range(chips)])
        out[plane, part : part + EXTRA] = tail[0]
        out[plane, part + EXTRA :] = tail[1]


def shards(hidden, head_weight, labels, loss_mask):
    weights = head_weight[0]
    words, feats = weights.shape
    place = jnp.stack([lax.axis_index(a) for a in ("core", "tok")]).astype(jnp.int32)
    first_word = lax.axis_index(("y", "x", "core", "tok")) * words
    word_ids = first_word + lax.broadcasted_iota(jnp.int32, (words, 1), 0)
    mask = loss_mask.astype(F32)

    block = hidden[0]
    rows, wide = block.shape
    half = 2 * rows
    array = jax.ShapeDtypeStruct
    turns = [
        lax.ppermute(block, "tok", [(i, (i + k) % 4) for i in range(4)]) for k in range(1, 4)
    ]
    halves = vmem_call(
        order_tok_kernel,
        [array((16, half, wide), BF16)] * 2,
        block,
        *turns,
        place=place,
        scratch=[pltpu.VMEM((4, rows, wide), BF16)],
    )

    own_z, sent = [], []
    for c in range(2):
        x = halves[c]
        if c == 1:
            x, own_z[0] = lax.optimization_barrier((x, own_z[0]))
        own_z.append(scores(place, weights, exchanged(x, CHIPS)))
        sent.append(lax.ppermute(own_z[c], "grp", [(0, 1)]))

    hits = [word_ids == labels[c * half : (c + 1) * half][None, :] for c in range(2)]
    stats = []
    for c in range(2):
        z = own_z[c].astype(F32)
        peak = jnp.max(z, axis=0)
        stats.append(
            jnp.stack(
                [
                    peak,
                    jnp.sum(jnp.exp(z - peak), axis=0),
                    jnp.sum(jnp.where(hits[c], z, 0.0), axis=0),
                ]
            )
        )
    stats = jnp.concatenate(stats, axis=1)
    stats = vmem_call(
        pair_kernel, array((16,) + stats.shape, F32), stats, swapped(stats, "core")
    )
    stats = vmem_call(
        chips_kernel, array((8,) + stats.shape[1:], F32), exchanged(stats, CHIPS)
    )
    norms = vmem_call(planes_kernel, array(stats.shape[1:], F32), exchanged(stats, PLANES))
    teacher_norm, student_norm, label_logit = norms

    parts = []
    for c in range(2):
        span = slice(c * half, (c + 1) * half)
        teacher_logp = sent[c].astype(F32) - teacher_norm[span]
        student_logp = own_z[c].astype(F32) - student_norm[span]
        teacher_prob = jnp.exp(teacher_logp)
        student_prob = jnp.exp(student_logp)
        diverge = jnp.sum(teacher_prob * (teacher_logp - student_logp), axis=0)
        grads = (
            (2.0 * student_prob - teacher_prob - hits[c].astype(F32)) * mask[span]
        ).astype(BF16)
        extra = jnp.zeros((EXTRA, wide), F32).at[:2].set(diverge.reshape(2, wide))
        parts.append(split_grads(place, weights, grads, extra))
    summed = []
    for keep, send in parts:
        paired = vmem_call(
            pair_sum_kernel, array(keep.shape, F32), keep, swapped_in_student(send)
        )
        summed.append(exchanged(paired, CHIPS))

    part = half // 4
    last = vmem_call(
        last_split_kernel, array((8, part + 2 * EXTRA, wide), F32), *summed
    )
    mine = total(list(exchanged(last, PLANES))[4:])
    input_grads = mine[:part].astype(BF16)
    diverged = jnp.concatenate([mine[part : part + 2], mine[part + EXTRA : part + EXTRA + 2]])
    token_loss = mask * (diverged.reshape(-1) + student_norm - label_logit)
    return (input_grads, token_loss, jnp.stack([teacher_norm, student_norm]))


def solution(mesh):
    fine = Mesh(mesh.devices.reshape(2, 4, 4, 2, 4), ("grp", "y", "x", "core", "tok"))
    vocab = ("y", "x", "core")
    return jax.shard_map(
        shards,
        mesh=fine,
        in_specs=(
            P("grp", "tok", vocab),
            P("grp", vocab + ("tok",), None),
            P(),
            P(),
        ),
        out_specs=(P(("grp", "tok"), vocab), P(), P()),
        check_vma=False,
    )
```

```python
import functools
import jax
import jax.numpy as jnp
from jax import lax
from jax.experimental import pallas as pl
from jax.experimental.pallas import tpu as pltpu
from jax.sharding import Mesh, PartitionSpec as P

BF16 = jnp.bfloat16
F32 = jnp.float32
MIB = 1024 * 1024
EXTRA = 8
STRIPS = 4
CHIPS = ("y", "x")
PLANES = ("grp", "tok")


def in_vmem():
    return pl.BlockSpec(memory_space=pltpu.VMEM)


def in_smem():
    return pl.BlockSpec(memory_space=pltpu.SMEM)


def vmem_call(kernel, out_shape, *arrays, place=None, weights=None, scratch=(), mib=12):
    scalars = [] if place is None else [place]
    remote = [] if weights is None else [weights]
    return pl.pallas_call(
        kernel,
        out_shape=out_shape,
        in_specs=[in_smem()] * len(scalars)
        + [pl.BlockSpec(memory_space=pl.ANY)] * len(remote)
        + [in_vmem()] * len(arrays),
        out_specs=jax.tree.map(lambda _: in_vmem(), out_shape),
        scratch_shapes=list(scratch),
        compiler_params=pltpu.CompilerParams(vmem_limit_bytes=mib * MIB),
    )(*scalars, *remote, *arrays)


def swapped(x, axis):
    return lax.ppermute(x, axis, [(0, 1), (1, 0)])


def swapped_in_student(x):
    return lax.ppermute(x, ("grp", "core"), [(2, 3), (3, 2)])


def exchanged(x, axes):
    return lax.all_to_all(x, axes, 0, 0)


def order_tok_kernel(place_ref, p0, p1, p2, p3, lower, upper, held):
    me = place_ref[1]
    rows = p0.shape[0]
    for k, piece in enumerate((p0, p1, p2, p3)):
        held[lax.rem(me + 4 - k, 4)] = piece[...]
    for chip in range(lower.shape[0]):
        lower[chip, :rows] = held[0]
        lower[chip, rows:] = held[1]
        upper[chip, :rows] = held[2]
        upper[chip, rows:] = held[3]


def strips_of(weights, held, sems):
    depth = held.shape[2]
    copies = [
        pltpu.make_async_copy(weights.at[:, pl.ds(i * depth, depth)], held.at[i], sems.at[i])
        for i in range(STRIPS)
    ]
    for copy in copies:
        copy.start()
    return copies


def scores_kernel(place_ref, weights, own, sibling, out, joined, held, acc, sems):
    core = place_ref[0]
    chips, _, wide = own.shape
    depth = held.shape[2]
    words = out.shape[0]
    copies = strips_of(weights, held, sems)

    def join(first, second):
        for chip in range(chips):
            at = 2 * chip * wide
            joined[:, at : at + wide] = first[chip]
            joined[:, at + wide : at + 2 * wide] = second[chip]

    @pl.when(core == 0)
    def _():
        join(own, sibling)

    @pl.when(core != 0)
    def _():
        join(sibling, own)

    tall = 608
    for i in range(STRIPS):
        copies[i].wait()
        for start in range(0, words, tall):
            at = slice(start, min(start + tall, words))
            part = lax.dot_general(
                held[i, at],
                joined[:, i * depth : (i + 1) * depth],
                (((1,), (1,)), ((), ())),
                preferred_element_type=F32,
            )
            if i > 0:
                part = acc[at] + part
            if i < STRIPS - 1:
                acc[at] = part
            else:
                out[at] = part.astype(BF16)


def scores(place, weights, own):
    words, feats = weights.shape
    tokens = own.shape[1]
    return vmem_call(
        scores_kernel,
        jax.ShapeDtypeStruct((words, tokens), BF16),
        own,
        swapped(own, "core"),
        place=place,
        weights=weights,
        scratch=[
            pltpu.VMEM((tokens, feats), BF16),
            pltpu.VMEM((STRIPS, words, feats // STRIPS), BF16),
            pltpu.VMEM((words, tokens), F32),
            pltpu.SemaphoreType.DMA((STRIPS,)),
        ],
        mib=22,
    )


def total(parts):
    parts = list(parts)
    while len(parts) > 1:
        parts = [a + b for a, b in zip(parts[::2], parts[1::2])]
    return parts[0]


def merge(parts):
    peak = functools.reduce(jnp.maximum, [p[0:1] for p in parts])
    mass = total([p[1:2] * jnp.exp(p[0:1] - peak) for p in parts])
    return peak, mass, total([p[2:3] for p in parts])


def pair_kernel(mine, other, out):
    merged = merge([mine[...], other[...]])
    for copy in range(out.shape[0]):
        for row in range(3):
            out[copy, row : row + 1] = merged[row]


def chips_kernel(parts, out):
    merged = merge([parts[i] for i in range(parts.shape[0])])
    for copy in range(out.shape[0]):
        for row in range(3):
            out[copy, row : row + 1] = merged[row]


def planes_kernel(parts, out):
    for group in range(2):
        peak, mass, label = merge([parts[4 * group + i] for i in range(4)])
        out[group : group + 1] = peak + jnp.log(mass)
    out[2:3] = label


def grads_kernel(place_ref, weights, grads, extra, keep, send, turned, held, sems):
    core = place_ref[0]
    tokens = grads.shape[1]
    chips, _, wide = keep.shape
    copies = strips_of(weights, held, sems)
    turned[...] = grads[...].T
    per_strip = chips // STRIPS
    for chip in range(chips):
        strip, at = chip // per_strip, (chip % per_strip) * 2 * wide
        if at == 0:
            copies[strip].wait()
        full = jnp.dot(
            turned[...], held[strip, :, at : at + 2 * wide], preferred_element_type=F32
        )
        low = full[:, :wide]
        high = full[:, wide:]
        keep[chip, :tokens] = jnp.where(core == 0, low, high)
        send[chip, :tokens] = jnp.where(core == 0, high, low)
        keep[chip, tokens:] = extra[...]
        send[chip, tokens:] = extra[...]


def split_grads(place, weights, grads, extra):
    words, tokens = grads.shape
    feats = weights.shape[1]
    wide = extra.shape[1]
    part = jax.ShapeDtypeStruct((feats // (2 * wide), tokens + EXTRA, wide), F32)
    return vmem_call(
        grads_kernel,
        [part] * 2,
        grads,
        extra,
        place=place,
        weights=weights,
        scratch=[
            pltpu.VMEM((tokens, words), BF16),
            pltpu.VMEM((STRIPS, words, feats // STRIPS), BF16),
            pltpu.SemaphoreType.DMA((STRIPS,)),
        ],
        mib=22,
    )


def pair_sum_kernel(keep, got, out):
    out[...] = keep[...] + got[...]


def last_split_kernel(lower, upper, out):
    rows = lower.shape[1] - EXTRA
    part = rows // 4
    chips = lower.shape[0]
    tail = [total([half[i, rows:] for i in range(chips)]) for half in (lower, upper)]
    for plane in range(8):
        half = lower if plane < 4 else upper
        at = slice((plane % 4) * part, (plane % 4 + 1) * part)
        out[plane, :part] = total([half[i, at] for i in range(chips)])
        out[plane, part : part + EXTRA] = tail[0]
        out[plane, part + EXTRA :] = tail[1]


def shards(hidden, head_weight, labels, loss_mask):
    weights = head_weight[0]
    words, feats = weights.shape
    place = jnp.stack([lax.axis_index(a) for a in ("core", "tok")]).astype(jnp.int32)
    first_word = lax.axis_index(("y", "x", "core", "tok")) * words
    word_ids = first_word + lax.broadcasted_iota(jnp.int32, (words, 1), 0)
    mask = loss_mask.astype(F32)

    block = hidden[0]
    rows, wide = block.shape
    half = 2 * rows
    array = jax.ShapeDtypeStruct
    turns = [
        lax.ppermute(block, "tok", [(i, (i + k) % 4) for i in range(4)]) for k in range(1, 4)
    ]
    halves = vmem_call(
        order_tok_kernel,
        [array((16, half, wide), BF16)] * 2,
        block,
        *turns,
        place=place,
        scratch=[pltpu.VMEM((4, rows, wide), BF16)],
    )

    own_z, sent = [], []
    for c in range(2):
        x = halves[c]
        if c == 1:
            x, own_z[0] = lax.optimization_barrier((x, own_z[0]))
        x = exchanged(x, CHIPS)
        if c == 1:
            x, sent[0] = lax.optimization_barrier((x, sent[0]))
        own_z.append(scores(place, weights, x))
        sent.append(lax.ppermute(own_z[c], "grp", [(0, 1)]))

    hits = [word_ids == labels[c * half : (c + 1) * half][None, :] for c in range(2)]
    stats = []
    for c in range(2):
        z = own_z[c].astype(F32)
        peak = jnp.max(z, axis=0)
        stats.append(
            jnp.stack(
                [
                    peak,
                    jnp.sum(jnp.exp(z - peak), axis=0),
                    jnp.sum(jnp.where(hits[c], z, 0.0), axis=0),
                ]
            )
        )
    stats = jnp.concatenate(stats, axis=1)
    stats = vmem_call(
        pair_kernel, array((16,) + stats.shape, F32), stats, swapped(stats, "core")
    )
    stats = vmem_call(
        chips_kernel, array((8,) + stats.shape[1:], F32), exchanged(stats, CHIPS)
    )
    norms = vmem_call(planes_kernel, array(stats.shape[1:], F32), exchanged(stats, PLANES))
    norms, sent[0], sent[1] = lax.optimization_barrier((norms, sent[0], sent[1]))
    teacher_norm, student_norm, label_logit = norms

    parts = []
    for c in range(2):
        span = slice(c * half, (c + 1) * half)
        teacher_logp = sent[c].astype(F32) - teacher_norm[span]
        student_logp = own_z[c].astype(F32) - student_norm[span]
        teacher_prob = jnp.exp(teacher_logp)
        student_prob = jnp.exp(student_logp)
        diverge = jnp.sum(teacher_prob * (teacher_logp - student_logp), axis=0)
        grads = (
            (2.0 * student_prob - teacher_prob - hits[c].astype(F32)) * mask[span]
        ).astype(BF16)
        extra = jnp.zeros((EXTRA, wide), F32).at[:2].set(diverge.reshape(2, wide))
        parts.append(split_grads(place, weights, grads, extra))
    summed = []
    for keep, send in parts:
        paired = vmem_call(
            pair_sum_kernel, array(keep.shape, F32), keep, swapped_in_student(send)
        )
        summed.append(exchanged(paired, CHIPS))

    part = half // 4
    last = vmem_call(
        last_split_kernel, array((8, part + 2 * EXTRA, wide), F32), *summed
    )
    mine = total(list(exchanged(last, PLANES))[4:])
    input_grads = mine[:part].astype(BF16)
    diverged = jnp.concatenate([mine[part : part + 2], mine[part + EXTRA : part + EXTRA + 2]])
    token_loss = mask * (diverged.reshape(-1) + student_norm - label_logit)
    return (input_grads, token_loss, jnp.stack([teacher_norm, student_norm]))


def solution(mesh):
    fine = Mesh(mesh.devices.reshape(2, 4, 4, 2, 4), ("grp", "y", "x", "core", "tok"))
    vocab = ("y", "x", "core")
    return jax.shard_map(
        shards,
        mesh=fine,
        in_specs=(
            P("grp", "tok", vocab),
            P("grp", vocab + ("tok",), None),
            P(),
            P(),
        ),
        out_specs=(P(("grp", "tok"), vocab), P(), P()),
        check_vma=False,
    )
```

```python
import functools
import jax
import jax.numpy as jnp
from jax import lax
from jax.experimental import pallas as pl
from jax.experimental.pallas import tpu as pltpu
from jax.sharding import Mesh, PartitionSpec as P

BF16 = jnp.bfloat16
F32 = jnp.float32
MIB = 1024 * 1024
EXTRA = 8
STRIPS = 4
CHIPS = ("y", "x")
PLANES = ("grp", "tok")


def in_vmem():
    return pl.BlockSpec(memory_space=pltpu.VMEM)


def in_smem():
    return pl.BlockSpec(memory_space=pltpu.SMEM)


def vmem_call(kernel, out_shape, *arrays, place=None, weights=None, scratch=(), mib=12):
    scalars = [] if place is None else [place]
    remote = [] if weights is None else [weights]
    return pl.pallas_call(
        kernel,
        out_shape=out_shape,
        in_specs=[in_smem()] * len(scalars)
        + [pl.BlockSpec(memory_space=pltpu.HBM)] * len(remote)
        + [in_vmem()] * len(arrays),
        out_specs=jax.tree.map(lambda _: in_vmem(), out_shape),
        scratch_shapes=list(scratch),
        compiler_params=pltpu.CompilerParams(vmem_limit_bytes=mib * MIB),
    )(*scalars, *remote, *arrays)


def swapped(x, axis):
    return lax.ppermute(x, axis, [(0, 1), (1, 0)])


def swapped_in_student(x):
    return lax.ppermute(x, ("grp", "core"), [(2, 3), (3, 2)])


def exchanged(x, axes):
    return lax.all_to_all(x, axes, 0, 0)


def order_tok_kernel(place_ref, p0, p1, p2, p3, lower, upper, held):
    me = place_ref[1]
    rows = p0.shape[0]
    for k, piece in enumerate((p0, p1, p2, p3)):
        held[lax.rem(me + 4 - k, 4)] = piece[...]
    for chip in range(lower.shape[0]):
        lower[chip, :rows] = held[0]
        lower[chip, rows:] = held[1]
        upper[chip, :rows] = held[2]
        upper[chip, rows:] = held[3]


def strips_of(weights, held, sems):
    depth = held.shape[2]
    copies = [
        pltpu.make_async_copy(weights.at[:, pl.ds(i * depth, depth)], held.at[i], sems.at[i])
        for i in range(STRIPS)
    ]
    for copy in copies:
        copy.start()
    return copies


def scores_kernel(place_ref, weights, own, sibling, out, joined, held, acc, sems):
    core = place_ref[0]
    chips, _, wide = own.shape
    depth = held.shape[2]
    words = out.shape[0]
    copies = strips_of(weights, held, sems)

    def join(first, second):
        for chip in range(chips):
            at = 2 * chip * wide
            joined[:, at : at + wide] = first[chip]
            joined[:, at + wide : at + 2 * wide] = second[chip]

    @pl.when(core == 0)
    def _():
        join(own, sibling)

    @pl.when(core != 0)
    def _():
        join(sibling, own)

    tall = 608
    for i in range(STRIPS):
        copies[i].wait()
        for start in range(0, words, tall):
            at = slice(start, min(start + tall, words))
            part = lax.dot_general(
                held[i, at],
                joined[:, i * depth : (i + 1) * depth],
                (((1,), (1,)), ((), ())),
                preferred_element_type=F32,
            )
            if i > 0:
                part = acc[at] + part
            if i < STRIPS - 1:
                acc[at] = part
            else:
                out[at] = part.astype(BF16)


def scores(place, weights, own):
    words, feats = weights.shape
    tokens = own.shape[1]
    return vmem_call(
        scores_kernel,
        jax.ShapeDtypeStruct((words, tokens), BF16),
        own,
        swapped(own, "core"),
        place=place,
        weights=weights,
        scratch=[
            pltpu.VMEM((tokens, feats), BF16),
            pltpu.VMEM((STRIPS, words, feats // STRIPS), BF16),
            pltpu.VMEM((words, tokens), F32),
            pltpu.SemaphoreType.DMA((STRIPS,)),
        ],
        mib=22,
    )


def total(parts):
    parts = list(parts)
    while len(parts) > 1:
        parts = [a + b for a, b in zip(parts[::2], parts[1::2])]
    return parts[0]


def merge(parts):
    peak = functools.reduce(jnp.maximum, [p[0:1] for p in parts])
    mass = total([p[1:2] * jnp.exp(p[0:1] - peak) for p in parts])
    return peak, mass, total([p[2:3] for p in parts])


def pair_kernel(mine, other, out):
    merged = merge([mine[...], other[...]])
    for copy in range(out.shape[0]):
        for row in range(3):
            out[copy, row : row + 1] = merged[row]


def chips_kernel(parts, out):
    merged = merge([parts[i] for i in range(parts.shape[0])])
    for copy in range(out.shape[0]):
        for row in range(3):
            out[copy, row : row + 1] = merged[row]


def planes_kernel(parts, out):
    for group in range(2):
        peak, mass, label = merge([parts[4 * group + i] for i in range(4)])
        out[group : group + 1] = peak + jnp.log(mass)
    out[2:3] = label


def grads_kernel(place_ref, weights, grads, extra, keep, send, turned, held, sems):
    core = place_ref[0]
    tokens = grads.shape[1]
    chips, _, wide = keep.shape
    copies = strips_of(weights, held, sems)
    turned[...] = grads[...].T
    per_strip = chips // STRIPS
    for chip in range(chips):
        strip, at = chip // per_strip, (chip % per_strip) * 2 * wide
        if at == 0:
            copies[strip].wait()
        full = jnp.dot(
            turned[...], held[strip, :, at : at + 2 * wide], preferred_element_type=F32
        )
        low = full[:, :wide]
        high = full[:, wide:]
        keep[chip, :tokens] = jnp.where(core == 0, low, high)
        send[chip, :tokens] = jnp.where(core == 0, high, low)
        keep[chip, tokens:] = extra[...]
        send[chip, tokens:] = extra[...]


def split_grads(place, weights, grads, extra):
    words, tokens = grads.shape
    feats = weights.shape[1]
    wide = extra.shape[1]
    part = jax.ShapeDtypeStruct((feats // (2 * wide), tokens + EXTRA, wide), F32)
    return vmem_call(
        grads_kernel,
        [part] * 2,
        grads,
        extra,
        place=place,
        weights=weights,
        scratch=[
            pltpu.VMEM((tokens, words), BF16),
            pltpu.VMEM((STRIPS, words, feats // STRIPS), BF16),
            pltpu.SemaphoreType.DMA((STRIPS,)),
        ],
        mib=22,
    )


def pair_sum_kernel(keep, got, out):
    out[...] = keep[...] + got[...]


def last_split_kernel(lower, upper, out):
    rows = lower.shape[1] - EXTRA
    part = rows // 4
    chips = lower.shape[0]
    tail = [total([half[i, rows:] for i in range(chips)]) for half in (lower, upper)]
    for plane in range(8):
        half = lower if plane < 4 else upper
        at = slice((plane % 4) * part, (plane % 4 + 1) * part)
        out[plane, :part] = total([half[i, at] for i in range(chips)])
        out[plane, part : part + EXTRA] = tail[0]
        out[plane, part + EXTRA :] = tail[1]


def shards(hidden, head_weight, labels, loss_mask):
    weights = pltpu.with_memory_space_constraint(head_weight[0], pltpu.HBM)
    words, feats = weights.shape
    place = jnp.stack([lax.axis_index(a) for a in ("core", "tok")]).astype(jnp.int32)
    first_word = lax.axis_index(("y", "x", "core", "tok")) * words
    word_ids = first_word + lax.broadcasted_iota(jnp.int32, (words, 1), 0)
    mask = loss_mask.astype(F32)

    block = hidden[0]
    rows, wide = block.shape
    half = 2 * rows
    array = jax.ShapeDtypeStruct
    turns = [
        lax.ppermute(block, "tok", [(i, (i + k) % 4) for i in range(4)]) for k in range(1, 4)
    ]
    halves = vmem_call(
        order_tok_kernel,
        [array((16, half, wide), BF16)] * 2,
        block,
        *turns,
        place=place,
        scratch=[pltpu.VMEM((4, rows, wide), BF16)],
    )

    own_z, sent = [], []
    for c in range(2):
        x = halves[c]
        if c == 1:
            x, own_z[0] = lax.optimization_barrier((x, own_z[0]))
        x = exchanged(x, CHIPS)
        own_z.append(scores(place, weights, x))
        sent.append(lax.ppermute(own_z[c], "grp", [(0, 1)]))

    hits = [word_ids == labels[c * half : (c + 1) * half][None, :] for c in range(2)]
    stats = []
    for c in range(2):
        z = own_z[c].astype(F32)
        peak = jnp.max(z, axis=0)
        stats.append(
            jnp.stack(
                [
                    peak,
                    jnp.sum(jnp.exp(z - peak), axis=0),
                    jnp.sum(jnp.where(hits[c], z, 0.0), axis=0),
                ]
            )
        )
    stats = jnp.concatenate(stats, axis=1)
    stats = vmem_call(
        pair_kernel, array((16,) + stats.shape, F32), stats, swapped(stats, "core")
    )
    stats, sent[0] = lax.optimization_barrier((stats, sent[0]))
    stats = vmem_call(
        chips_kernel, array((8,) + stats.shape[1:], F32), exchanged(stats, CHIPS)
    )
    norms = vmem_call(planes_kernel, array(stats.shape[1:], F32), exchanged(stats, PLANES))
    norms, sent[0], sent[1] = lax.optimization_barrier((norms, sent[0], sent[1]))
    teacher_norm, student_norm, label_logit = norms

    parts = []
    for c in range(2):
        span = slice(c * half, (c + 1) * half)
        teacher_logp = sent[c].astype(F32) - teacher_norm[span]
        student_logp = own_z[c].astype(F32) - student_norm[span]
        teacher_prob = jnp.exp(teacher_logp)
        student_prob = jnp.exp(student_logp)
        diverge = jnp.sum(teacher_prob * (teacher_logp - student_logp), axis=0)
        grads = (
            (2.0 * student_prob - teacher_prob - hits[c].astype(F32)) * mask[span]
        ).astype(BF16)
        extra = jnp.zeros((EXTRA, wide), F32).at[:2].set(diverge.reshape(2, wide))
        parts.append(split_grads(place, weights, grads, extra))
    summed = []
    for keep, send in parts:
        paired = vmem_call(
            pair_sum_kernel, array(keep.shape, F32), keep, swapped_in_student(send)
        )
        summed.append(exchanged(paired, CHIPS))

    part = half // 4
    last = vmem_call(
        last_split_kernel, array((8, part + 2 * EXTRA, wide), F32), *summed
    )
    mine = total(list(exchanged(last, PLANES))[4:])
    input_grads = mine[:part].astype(BF16)
    diverged = jnp.concatenate([mine[part : part + 2], mine[part + EXTRA : part + EXTRA + 2]])
    token_loss = mask * (diverged.reshape(-1) + student_norm - label_logit)
    return (input_grads, token_loss, jnp.stack([teacher_norm, student_norm]))


def solution(mesh):
    fine = Mesh(mesh.devices.reshape(2, 4, 4, 2, 4), ("grp", "y", "x", "core", "tok"))
    vocab = ("y", "x", "core")
    return jax.shard_map(
        shards,
        mesh=fine,
        in_specs=(
            P("grp", "tok", vocab),
            P("grp", vocab + ("tok",), None),
            P(),
            P(),
        ),
        out_specs=(P(("grp", "tok"), vocab), P(), P()),
        check_vma=False,
    )
```

```python
import functools
import jax
import jax.numpy as jnp
from jax import lax
from jax.experimental import pallas as pl
from jax.experimental.pallas import tpu as pltpu
from jax.sharding import Mesh, PartitionSpec as P

BF16 = jnp.bfloat16
F32 = jnp.float32
MIB = 1024 * 1024
EXTRA = 8
STRIPS = 4
CHIPS = ("y", "x")
PLANES = ("grp", "tok")


def in_vmem():
    return pl.BlockSpec(memory_space=pltpu.VMEM)


def in_smem():
    return pl.BlockSpec(memory_space=pltpu.SMEM)


def vmem_call(kernel, out_shape, *arrays, place=None, weights=None, scratch=(), mib=12):
    scalars = [] if place is None else [place]
    remote = [] if weights is None else [weights]
    return pl.pallas_call(
        kernel,
        out_shape=out_shape,
        in_specs=[in_smem()] * len(scalars)
        + [pl.BlockSpec(memory_space=pltpu.HBM)] * len(remote)
        + [in_vmem()] * len(arrays),
        out_specs=jax.tree.map(lambda _: in_vmem(), out_shape),
        scratch_shapes=list(scratch),
        compiler_params=pltpu.CompilerParams(vmem_limit_bytes=mib * MIB),
    )(*scalars, *remote, *arrays)


def swapped(x, axis):
    return lax.ppermute(x, axis, [(0, 1), (1, 0)])


def swapped_in_student(x):
    return lax.ppermute(x, ("grp", "core"), [(2, 3), (3, 2)])


def exchanged(x, axes):
    return lax.all_to_all(x, axes, 0, 0)


def order_tok_kernel(place_ref, p0, p1, p2, p3, out, held):
    me = place_ref[1]
    rows = p0.shape[0]
    for k, piece in enumerate((p0, p1, p2, p3)):
        held[lax.rem(me + 4 - k, 4)] = piece[...]
    for chip in range(out.shape[0]):
        for j in range(4):
            out[chip, j * rows : (j + 1) * rows] = held[j]


def strips_of(weights, held, sems):
    depth = held.shape[2]
    copies = [
        pltpu.make_async_copy(weights.at[:, pl.ds(i * depth, depth)], held.at[i], sems.at[i])
        for i in range(STRIPS)
    ]
    for copy in copies:
        copy.start()
    return copies


def scores_kernel(half, place_ref, weights, own, sibling, out, joined, held, acc, sems):
    core = place_ref[0]
    chips, _, wide = own.shape
    tokens = out.shape[1]
    rows = slice(half * tokens, (half + 1) * tokens)
    depth = held.shape[2]
    words = out.shape[0]
    copies = strips_of(weights, held, sems)

    def join(first, second):
        for chip in range(chips):
            at = 2 * chip * wide
            joined[:, at : at + wide] = first[chip, rows]
            joined[:, at + wide : at + 2 * wide] = second[chip, rows]

    @pl.when(core == 0)
    def _():
        join(own, sibling)

    @pl.when(core != 0)
    def _():
        join(sibling, own)

    tall = 608
    for i in range(STRIPS):
        copies[i].wait()
        for start in range(0, words, tall):
            at = slice(start, min(start + tall, words))
            part = lax.dot_general(
                held[i, at],
                joined[:, i * depth : (i + 1) * depth],
                (((1,), (1,)), ((), ())),
                preferred_element_type=F32,
            )
            if i > 0:
                part = acc[at] + part
            if i < STRIPS - 1:
                acc[at] = part
            else:
                out[at] = part.astype(BF16)


def scores(place, weights, own, sibling, half):
    words, feats = weights.shape
    tokens = own.shape[1] // 2
    return vmem_call(
        functools.partial(scores_kernel, half),
        jax.ShapeDtypeStruct((words, tokens), BF16),
        own,
        sibling,
        place=place,
        weights=weights,
        scratch=[
            pltpu.VMEM((tokens, feats), BF16),
            pltpu.VMEM((STRIPS, words, feats // STRIPS), BF16),
            pltpu.VMEM((words, tokens), F32),
            pltpu.SemaphoreType.DMA((STRIPS,)),
        ],
        mib=22,
    )


def total(parts):
    parts = list(parts)
    while len(parts) > 1:
        parts = [a + b for a, b in zip(parts[::2], parts[1::2])]
    return parts[0]


def merge(parts):
    peak = functools.reduce(jnp.maximum, [p[0:1] for p in parts])
    mass = total([p[1:2] * jnp.exp(p[0:1] - peak) for p in parts])
    return peak, mass, total([p[2:3] for p in parts])


def pair_kernel(mine, other, out):
    merged = merge([mine[...], other[...]])
    for copy in range(out.shape[0]):
        for row in range(3):
            out[copy, row : row + 1] = merged[row]


def chips_kernel(parts, out):
    merged = merge([parts[i] for i in range(parts.shape[0])])
    for copy in range(out.shape[0]):
        for row in range(3):
            out[copy, row : row + 1] = merged[row]


def planes_kernel(parts, out):
    for group in range(2):
        peak, mass, label = merge([parts[4 * group + i] for i in range(4)])
        out[group : group + 1] = peak + jnp.log(mass)
    out[2:3] = label


def grads_kernel(place_ref, weights, grads, extra, keep, send, turned, held, sems):
    core = place_ref[0]
    tokens = grads.shape[1]
    chips, _, wide = keep.shape
    copies = strips_of(weights, held, sems)
    turned[...] = grads[...].T
    per_strip = chips // STRIPS
    for chip in range(chips):
        strip, at = chip // per_strip, (chip % per_strip) * 2 * wide
        if at == 0:
            copies[strip].wait()
        full = jnp.dot(
            turned[...], held[strip, :, at : at + 2 * wide], preferred_element_type=F32
        )
        low = full[:, :wide]
        high = full[:, wide:]
        keep[chip, :tokens] = jnp.where(core == 0, low, high)
        send[chip, :tokens] = jnp.where(core == 0, high, low)
        keep[chip, tokens:] = extra[...]
        send[chip, tokens:] = extra[...]


def split_grads(place, weights, grads, extra):
    words, tokens = grads.shape
    feats = weights.shape[1]
    wide = extra.shape[1]
    part = jax.ShapeDtypeStruct((feats // (2 * wide), tokens + EXTRA, wide), F32)
    return vmem_call(
        grads_kernel,
        [part] * 2,
        grads,
        extra,
        place=place,
        weights=weights,
        scratch=[
            pltpu.VMEM((tokens, words), BF16),
            pltpu.VMEM((STRIPS, words, feats // STRIPS), BF16),
            pltpu.SemaphoreType.DMA((STRIPS,)),
        ],
        mib=22,
    )


def line_total(parts):
    return (parts[0] + parts[2]) + (parts[1] + parts[3])


def pair_sum_kernel(x_first, place_ref, keep, got, *outs):
    y, x = place_ref[2], place_ref[3]
    rows = keep.shape[1] - EXTRA
    for first, out in enumerate(outs):
        for second in range(4):
            kx, ky = (first, second) if x_first else (second, first)
            chip = lax.rem(y + ky, 4) * 4 + lax.rem(x + kx, 4)
            at = slice(second * rows, (second + 1) * rows)
            out[at] = keep[chip, :rows] + got[chip, :rows]
        out[4 * rows :] = keep[0, rows:] + got[0, rows:]


def line_sum_kernel(p0, p1, p2, p3, *outs):
    parts = (p0, p1, p2, p3)
    rows = outs[0].shape[0] - EXTRA
    extra = line_total([p[4 * rows :] for p in parts])
    for k, out in enumerate(outs):
        at = slice(k * rows, (k + 1) * rows)
        out[:rows] = line_total([p[at] for p in parts])
        out[rows:] = extra


def last_split_kernel(a0, a1, a2, a3, b0, b1, b2, b3, out):
    halves = ((a0, a1, a2, a3), (b0, b1, b2, b3))
    rows = a0.shape[0] - EXTRA
    part = rows // 4
    tails = [line_total([p[rows:] for p in half]) for half in halves]
    for plane in range(8):
        at = slice((plane % 4) * part, (plane % 4 + 1) * part)
        out[plane, :part] = line_total([p[at] for p in halves[plane // 4]])
        out[plane, part : part + EXTRA] = tails[0]
        out[plane, part + EXTRA :] = tails[1]


def scattered(parts, axis):
    def moved(part, step):
        return lax.ppermute(part, axis, [(i, (i + step) % 4) for i in range(4)])

    return [parts[0]] + [moved(parts[k], k) for k in range(1, 4)]


def shards(hidden, head_weight, labels, loss_mask):
    weights = pltpu.with_memory_space_constraint(head_weight[0], pltpu.HBM)
    words, feats = weights.shape
    place = jnp.stack([lax.axis_index(a) for a in ("core", "tok", "y", "x")]).astype(jnp.int32)
    first_word = lax.axis_index(("y", "x", "core", "tok")) * words
    word_ids = first_word + lax.broadcasted_iota(jnp.int32, (words, 1), 0)
    mask = loss_mask.astype(F32)

    block = hidden[0]
    rows, wide = block.shape
    half = 2 * rows
    array = jax.ShapeDtypeStruct
    turns = [
        lax.ppermute(block, "tok", [(i, (i + k) % 4) for i in range(4)]) for k in range(1, 4)
    ]
    own = vmem_call(
        order_tok_kernel,
        array((16, 2 * half, wide), BF16),
        block,
        *turns,
        place=place,
        scratch=[pltpu.VMEM((4, rows, wide), BF16)],
    )
    own = exchanged(own, CHIPS)
    sibling = swapped(own, "core")
    own_z, sent = [], []
    for c in range(2):
        own_z.append(scores(place, weights, own, sibling, c))
        sent.append(lax.ppermute(own_z[c], "grp", [(0, 1)]))
        if c == 0:
            sibling, own_z[0] = lax.optimization_barrier((sibling, own_z[0]))

    hits = [word_ids == labels[c * half : (c + 1) * half][None, :] for c in range(2)]
    stats = []
    for c in range(2):
        z = own_z[c].astype(F32)
        peak = jnp.max(z, axis=0)
        stats.append(
            jnp.stack(
                [
                    peak,
                    jnp.sum(jnp.exp(z - peak), axis=0),
                    jnp.sum(jnp.where(hits[c], z, 0.0), axis=0),
                ]
            )
        )
    stats = jnp.concatenate(stats, axis=1)
    stats = vmem_call(
        pair_kernel, array((16,) + stats.shape, F32), stats, swapped(stats, "core")
    )
    stats = vmem_call(
        chips_kernel, array((8,) + stats.shape[1:], F32), exchanged(stats, CHIPS)
    )
    norms = vmem_call(planes_kernel, array(stats.shape[1:], F32), exchanged(stats, PLANES))
    norms, sent[0], sent[1] = lax.optimization_barrier((norms, sent[0], sent[1]))
    teacher_norm, student_norm, label_logit = norms

    parts = []
    for c in range(2):
        span = slice(c * half, (c + 1) * half)
        teacher_logp = sent[c].astype(F32) - teacher_norm[span]
        student_logp = own_z[c].astype(F32) - student_norm[span]
        teacher_prob = jnp.exp(teacher_logp)
        student_prob = jnp.exp(student_logp)
        diverge = jnp.sum(teacher_prob * (teacher_logp - student_logp), axis=0)
        grads = (
            (2.0 * student_prob - teacher_prob - hits[c].astype(F32)) * mask[span]
        ).astype(BF16)
        extra = jnp.zeros((EXTRA, wide), F32).at[:2].set(diverge.reshape(2, wide))
        parts.append(split_grads(place, weights, grads, extra))
    orders = (("x", "y"), ("y", "x"))
    array_of = lambda rows: [array((rows + EXTRA, wide), F32)] * 4
    pieces = [
        vmem_call(
            functools.partial(pair_sum_kernel, c == 0),
            array_of(4 * half),
            keep,
            swapped_in_student(send),
            place=place,
        )
        for c, (keep, send) in enumerate(parts)
    ]
    pieces = [scattered(pieces[c], orders[c][0]) for c in range(2)]
    pieces = [vmem_call(line_sum_kernel, array_of(half), *pieces[c]) for c in range(2)]
    pieces = [scattered(pieces[c], orders[c][1]) for c in range(2)]

    part = half // 4
    last = vmem_call(
        last_split_kernel,
        array((8, part + 2 * EXTRA, wide), F32),
        *pieces[0],
        *pieces[1],
    )
    mine = total(list(exchanged(last, PLANES))[4:])
    input_grads = mine[:part].astype(BF16)
    diverged = jnp.concatenate([mine[part : part + 2], mine[part + EXTRA : part + EXTRA + 2]])
    token_loss = mask * (diverged.reshape(-1) + student_norm - label_logit)
    return (input_grads, token_loss, jnp.stack([teacher_norm, student_norm]))


def solution(mesh):
    fine = Mesh(mesh.devices.reshape(2, 4, 4, 2, 4), ("grp", "y", "x", "core", "tok"))
    vocab = ("y", "x", "core")
    return jax.shard_map(
        shards,
        mesh=fine,
        in_specs=(
            P("grp", "tok", vocab),
            P("grp", vocab + ("tok",), None),
            P(),
            P(),
        ),
        out_specs=(P(("grp", "tok"), vocab), P(), P()),
        check_vma=False,
    )
```

```python
import functools
import jax
import jax.numpy as jnp
from jax import lax
from jax.experimental import pallas as pl
from jax.experimental.pallas import tpu as pltpu
from jax.sharding import Mesh, PartitionSpec as P

BF16 = jnp.bfloat16
F32 = jnp.float32
MIB = 1024 * 1024
EXTRA = 8
STRIPS = 4
CHIPS = ("y", "x")
PLANES = ("grp", "tok")


def in_vmem():
    return pl.BlockSpec(memory_space=pltpu.VMEM)


def in_smem():
    return pl.BlockSpec(memory_space=pltpu.SMEM)


def vmem_call(kernel, out_shape, *arrays, place=None, weights=None, scratch=(), mib=12):
    scalars = [] if place is None else [place]
    remote = [] if weights is None else [weights]
    return pl.pallas_call(
        kernel,
        out_shape=out_shape,
        in_specs=[in_smem()] * len(scalars)
        + [pl.BlockSpec(memory_space=pltpu.HBM)] * len(remote)
        + [in_vmem()] * len(arrays),
        out_specs=jax.tree.map(lambda _: in_vmem(), out_shape),
        scratch_shapes=list(scratch),
        compiler_params=pltpu.CompilerParams(vmem_limit_bytes=mib * MIB),
    )(*scalars, *remote, *arrays)


def swapped(x, axis):
    return lax.ppermute(x, axis, [(0, 1), (1, 0)])


def swapped_in_student(x):
    return lax.ppermute(x, ("grp", "core"), [(2, 3), (3, 2)])


def exchanged(x, axes):
    return lax.all_to_all(x, axes, 0, 0)


def order_tok_kernel(place_ref, p0, p1, p2, p3, out, held):
    me = place_ref[1]
    rows = p0.shape[0]
    for k, piece in enumerate((p0, p1, p2, p3)):
        held[lax.rem(me + 4 - k, 4)] = piece[...]
    for chip in range(out.shape[0]):
        for j in range(4):
            out[chip, j * rows : (j + 1) * rows] = held[j]


def strips_of(weights, held, sems):
    depth = held.shape[2]
    copies = [
        pltpu.make_async_copy(weights.at[:, pl.ds(i * depth, depth)], held.at[i], sems.at[i])
        for i in range(STRIPS)
    ]
    for copy in copies:
        copy.start()
    return copies


def scores_kernel(half, place_ref, weights, own, sibling, out, joined, held, acc, sems):
    core = place_ref[0]
    chips, _, wide = own.shape
    tokens = out.shape[1]
    rows = slice(half * tokens, (half + 1) * tokens)
    depth = held.shape[2]
    words = out.shape[0]
    copies = strips_of(weights, held, sems)

    def join(first, second):
        for chip in range(chips):
            at = 2 * chip * wide
            joined[:, at : at + wide] = first[chip, rows]
            joined[:, at + wide : at + 2 * wide] = second[chip, rows]

    @pl.when(core == 0)
    def _():
        join(own, sibling)

    @pl.when(core != 0)
    def _():
        join(sibling, own)

    tall = 608
    for i in range(STRIPS):
        copies[i].wait()
        for start in range(0, words, tall):
            at = slice(start, min(start + tall, words))
            part = lax.dot_general(
                held[i, at],
                joined[:, i * depth : (i + 1) * depth],
                (((1,), (1,)), ((), ())),
                preferred_element_type=F32,
            )
            if i > 0:
                part = acc[at] + part
            if i < STRIPS - 1:
                acc[at] = part
            else:
                out[at] = part.astype(BF16)


def scores(place, weights, own, sibling, half):
    words, feats = weights.shape
    tokens = own.shape[1] // 2
    return vmem_call(
        functools.partial(scores_kernel, half),
        jax.ShapeDtypeStruct((words, tokens), BF16),
        own,
        sibling,
        place=place,
        weights=weights,
        scratch=[
            pltpu.VMEM((tokens, feats), BF16),
            pltpu.VMEM((STRIPS, words, feats // STRIPS), BF16),
            pltpu.VMEM((words, tokens), F32),
            pltpu.SemaphoreType.DMA((STRIPS,)),
        ],
        mib=22,
    )


def total(parts):
    parts = list(parts)
    while len(parts) > 1:
        parts = [a + b for a, b in zip(parts[::2], parts[1::2])]
    return parts[0]


def merge(parts):
    peak = functools.reduce(jnp.maximum, [p[0:1] for p in parts])
    mass = total([p[1:2] * jnp.exp(p[0:1] - peak) for p in parts])
    return peak, mass, total([p[2:3] for p in parts])


def pair_kernel(mine, other, out):
    merged = merge([mine[...], other[...]])
    for copy in range(out.shape[0]):
        for row in range(3):
            out[copy, row : row + 1] = merged[row]


def chips_kernel(parts, out):
    merged = merge([parts[i] for i in range(parts.shape[0])])
    for copy in range(out.shape[0]):
        for row in range(3):
            out[copy, row : row + 1] = merged[row]


def planes_kernel(parts, out):
    for group in range(2):
        peak, mass, label = merge([parts[4 * group + i] for i in range(4)])
        out[group : group + 1] = peak + jnp.log(mass)
    out[2:3] = label


def grads_kernel(place_ref, weights, grads, extra, keep, send, turned, held, sems):
    core = place_ref[0]
    tokens = grads.shape[1]
    chips, _, wide = keep.shape
    copies = strips_of(weights, held, sems)
    turned[...] = grads[...].T
    per_strip = chips // STRIPS
    for chip in range(chips):
        strip, at = chip // per_strip, (chip % per_strip) * 2 * wide
        if at == 0:
            copies[strip].wait()
        full = jnp.dot(
            turned[...], held[strip, :, at : at + 2 * wide], preferred_element_type=F32
        )
        low = full[:, :wide]
        high = full[:, wide:]
        keep[chip, :tokens] = jnp.where(core == 0, low, high)
        send[chip, :tokens] = jnp.where(core == 0, high, low)
        keep[chip, tokens:] = extra[...]
        send[chip, tokens:] = extra[...]


def split_grads(place, weights, grads, extra):
    words, tokens = grads.shape
    feats = weights.shape[1]
    wide = extra.shape[1]
    part = jax.ShapeDtypeStruct((feats // (2 * wide), tokens + EXTRA, wide), F32)
    return vmem_call(
        grads_kernel,
        [part] * 2,
        grads,
        extra,
        place=place,
        weights=weights,
        scratch=[
            pltpu.VMEM((tokens, words), BF16),
            pltpu.VMEM((STRIPS, words, feats // STRIPS), BF16),
            pltpu.SemaphoreType.DMA((STRIPS,)),
        ],
        mib=22,
    )


def line_total(parts):
    return (parts[0] + parts[2]) + (parts[1] + parts[3])


def pair_sum_kernel(x_first, place_ref, keep, got, stay, right, left, ahead, behind):
    y, x = place_ref[2], place_ref[3]
    rows = keep.shape[1] - EXTRA
    extra = keep[0, rows:] + got[0, rows:]
    for first in range(4):
        for second in range(4):
            kx, ky = (first, second) if x_first else (second, first)
            chip = lax.rem(y + ky, 4) * 4 + lax.rem(x + kx, 4)
            if first == 2:
                out, slot = (ahead, second) if second < 2 else (behind, second - 2)
            else:
                out, slot = (stay, right, None, left)[first], second
            at = slice(slot * rows, (slot + 1) * rows)
            out[at] = keep[chip, :rows] + got[chip, :rows]
    stay[4 * rows :] = extra
    ahead[2 * rows :] = extra


def relay_kernel(stay, right, left, ahead, behind, to_right, to_left):
    rows = right.shape[0]
    half = rows // 2
    to_right[:half] = right[:half] + ahead[:half]
    to_right[half:rows] = right[half:]
    to_right[rows : rows + EXTRA] = stay[rows:]
    to_right[rows + EXTRA :] = ahead[half:]
    to_left[:half] = left[:half]
    to_left[half:rows] = left[half:] + behind[...]
    to_left[rows:] = stay[rows:]


def line_sum_kernel(stay, from_left, from_right, *outs):
    rows = outs[0].shape[0] - EXTRA
    end = 4 * rows
    near = from_left[end : end + EXTRA] + from_right[end:]
    extra = (stay[end:] + from_left[end + EXTRA :]) + near
    for k, out in enumerate(outs):
        at = slice(k * rows, (k + 1) * rows)
        out[:rows] = stay[at] + (from_left[at] + from_right[at])
        out[rows:] = extra


def last_split_kernel(a0, a1, a2, a3, b0, b1, b2, b3, out):
    halves = ((a0, a1, a2, a3), (b0, b1, b2, b3))
    rows = a0.shape[0] - EXTRA
    part = rows // 4
    tails = [line_total([p[rows:] for p in half]) for half in halves]
    for plane in range(8):
        at = slice((plane % 4) * part, (plane % 4 + 1) * part)
        out[plane, :part] = line_total([p[at] for p in halves[plane // 4]])
        out[plane, part : part + EXTRA] = tails[0]
        out[plane, part + EXTRA :] = tails[1]


def moved(part, axis, step):
    return lax.ppermute(part, axis, [(i, (i + step) % 4) for i in range(4)])


def shards(hidden, head_weight, labels, loss_mask):
    weights = pltpu.with_memory_space_constraint(head_weight[0], pltpu.HBM)
    words, feats = weights.shape
    place = jnp.stack([lax.axis_index(a) for a in ("core", "tok", "y", "x")]).astype(jnp.int32)
    first_word = lax.axis_index(("y", "x", "core", "tok")) * words
    word_ids = first_word + lax.broadcasted_iota(jnp.int32, (words, 1), 0)
    mask = loss_mask.astype(F32)

    block = hidden[0]
    rows, wide = block.shape
    half = 2 * rows
    array = jax.ShapeDtypeStruct
    turns = [
        lax.ppermute(block, "tok", [(i, (i + k) % 4) for i in range(4)]) for k in range(1, 4)
    ]
    own = vmem_call(
        order_tok_kernel,
        array((16, 2 * half, wide), BF16),
        block,
        *turns,
        place=place,
        scratch=[pltpu.VMEM((4, rows, wide), BF16)],
    )
    own = exchanged(own, CHIPS)
    sibling = swapped(own, "core")
    own_z, sent = [], []
    for c in range(2):
        own_z.append(scores(place, weights, own, sibling, c))
        sent.append(lax.ppermute(own_z[c], "grp", [(0, 1)]))
        if c == 0:
            sibling, own_z[0] = lax.optimization_barrier((sibling, own_z[0]))

    hits = [word_ids == labels[c * half : (c + 1) * half][None, :] for c in range(2)]
    stats = []
    for c in range(2):
        z = own_z[c].astype(F32)
        peak = jnp.max(z, axis=0)
        stats.append(
            jnp.stack(
                [
                    peak,
                    jnp.sum(jnp.exp(z - peak), axis=0),
                    jnp.sum(jnp.where(hits[c], z, 0.0), axis=0),
                ]
            )
        )
    stats = jnp.concatenate(stats, axis=1)
    stats = vmem_call(
        pair_kernel, array((16,) + stats.shape, F32), stats, swapped(stats, "core")
    )
    stats = vmem_call(
        chips_kernel, array((8,) + stats.shape[1:], F32), exchanged(stats, CHIPS)
    )
    norms = vmem_call(planes_kernel, array(stats.shape[1:], F32), exchanged(stats, PLANES))
    norms, sent[0], sent[1] = lax.optimization_barrier((norms, sent[0], sent[1]))
    teacher_norm, student_norm, label_logit = norms

    parts = []
    for c in range(2):
        span = slice(c * half, (c + 1) * half)
        teacher_logp = sent[c].astype(F32) - teacher_norm[span]
        student_logp = own_z[c].astype(F32) - student_norm[span]
        teacher_prob = jnp.exp(teacher_logp)
        student_prob = jnp.exp(student_logp)
        diverge = jnp.sum(teacher_prob * (teacher_logp - student_logp), axis=0)
        grads = (
            (2.0 * student_prob - teacher_prob - hits[c].astype(F32)) * mask[span]
        ).astype(BF16)
        extra = jnp.zeros((EXTRA, wide), F32).at[:2].set(diverge.reshape(2, wide))
        parts.append(split_grads(place, weights, grads, extra))
    orders = (("x", "y"), ("y", "x"))
    arrays = lambda *heights: [array((height, wide), F32) for height in heights]
    full, edge = 4 * half, EXTRA
    pieces = [
        vmem_call(
            functools.partial(pair_sum_kernel, c == 0),
            arrays(full + edge, full, full, full // 2 + edge, full // 2),
            keep,
            swapped_in_student(send),
            place=place,
        )
        for c, (keep, send) in enumerate(parts)
    ]
    relayed = []
    for c, (stay, right, left, ahead, behind) in enumerate(pieces):
        axis = orders[c][0]
        relayed.append(
            vmem_call(
                relay_kernel,
                arrays(full + 2 * edge, full + edge),
                stay,
                right,
                left,
                moved(ahead, axis, 1),
                moved(behind, axis, 3),
            )
        )
    lines = []
    for c, (to_right, to_left) in enumerate(relayed):
        axis = orders[c][0]
        lines.append(
            vmem_call(
                line_sum_kernel,
                arrays(*[half + edge] * 4),
                pieces[c][0],
                moved(to_right, axis, 1),
                moved(to_left, axis, 3),
            )
        )
    pieces = [
        [lines[c][0]] + [moved(lines[c][k], orders[c][1], k) for k in range(1, 4)]
        for c in range(2)
    ]

    part = half // 4
    last = vmem_call(
        last_split_kernel,
        array((8, part + 2 * EXTRA, wide), F32),
        *pieces[0],
        *pieces[1],
    )
    mine = total(list(exchanged(last, PLANES))[4:])
    input_grads = mine[:part].astype(BF16)
    diverged = jnp.concatenate([mine[part : part + 2], mine[part + EXTRA : part + EXTRA + 2]])
    token_loss = mask * (diverged.reshape(-1) + student_norm - label_logit)
    return (input_grads, token_loss, jnp.stack([teacher_norm, student_norm]))


def solution(mesh):
    fine = Mesh(mesh.devices.reshape(2, 4, 4, 2, 4), ("grp", "y", "x", "core", "tok"))
    vocab = ("y", "x", "core")
    return jax.shard_map(
        shards,
        mesh=fine,
        in_specs=(
            P("grp", "tok", vocab),
            P("grp", vocab + ("tok",), None),
            P(),
            P(),
        ),
        out_specs=(P(("grp", "tok"), vocab), P(), P()),
        check_vma=False,
    )
```

```python
import functools
import jax
import jax.numpy as jnp
from jax import lax
from jax.experimental import pallas as pl
from jax.experimental.pallas import tpu as pltpu
from jax.sharding import Mesh, PartitionSpec as P

BF16 = jnp.bfloat16
F32 = jnp.float32
MIB = 1024 * 1024
EXTRA = 8
STRIPS = 4
CHIPS = ("y", "x")
PLANES = ("grp", "tok")


def in_vmem():
    return pl.BlockSpec(memory_space=pltpu.VMEM)


def in_smem():
    return pl.BlockSpec(memory_space=pltpu.SMEM)


def vmem_call(kernel, out_shape, *arrays, place=None, weights=None, scratch=(), mib=12):
    scalars = [] if place is None else [place]
    remote = [] if weights is None else [weights]
    return pl.pallas_call(
        kernel,
        out_shape=out_shape,
        in_specs=[in_smem()] * len(scalars)
        + [pl.BlockSpec(memory_space=pltpu.HBM)] * len(remote)
        + [in_vmem()] * len(arrays),
        out_specs=jax.tree.map(lambda _: in_vmem(), out_shape),
        scratch_shapes=list(scratch),
        compiler_params=pltpu.CompilerParams(vmem_limit_bytes=mib * MIB),
    )(*scalars, *remote, *arrays)


def swapped(x, axis):
    return lax.ppermute(x, axis, [(0, 1), (1, 0)])


def exchanged(x, axes):
    return lax.all_to_all(x, axes, 0, 0)


def order_tok_kernel(place_ref, p0, p1, p2, p3, out, held):
    me = place_ref[1]
    rows = p0.shape[0]
    for k, piece in enumerate((p0, p1, p2, p3)):
        held[lax.rem(me + 4 - k, 4)] = piece[...]
    for chip in range(out.shape[0]):
        for j in range(4):
            out[chip, j * rows : (j + 1) * rows] = held[j]


def strips_of(weights, held, sems):
    depth = held.shape[2]
    copies = [
        pltpu.make_async_copy(weights.at[:, pl.ds(i * depth, depth)], held.at[i], sems.at[i])
        for i in range(STRIPS)
    ]
    for copy in copies:
        copy.start()
    return copies


def scores_kernel(half, place_ref, weights, own, sibling, out, joined, held, acc, sems):
    core = place_ref[0]
    chips, _, wide = own.shape
    tokens = out.shape[1]
    rows = slice(half * tokens, (half + 1) * tokens)
    depth = held.shape[2]
    words = out.shape[0]
    copies = strips_of(weights, held, sems)

    def join(first, second):
        for chip in range(chips):
            at = 2 * chip * wide
            joined[:, at : at + wide] = first[chip, rows]
            joined[:, at + wide : at + 2 * wide] = second[chip, rows]

    @pl.when(core == 0)
    def _():
        join(own, sibling)

    @pl.when(core != 0)
    def _():
        join(sibling, own)

    tall = 608
    for i in range(STRIPS):
        copies[i].wait()
        for start in range(0, words, tall):
            at = slice(start, min(start + tall, words))
            part = lax.dot_general(
                held[i, at],
                joined[:, i * depth : (i + 1) * depth],
                (((1,), (1,)), ((), ())),
                preferred_element_type=F32,
            )
            if i > 0:
                part = acc[at] + part
            if i < STRIPS - 1:
                acc[at] = part
            else:
                out[at] = part.astype(BF16)


def scores(place, weights, own, sibling, half):
    words, feats = weights.shape
    tokens = own.shape[1] // 2
    return vmem_call(
        functools.partial(scores_kernel, half),
        jax.ShapeDtypeStruct((words, tokens), BF16),
        own,
        sibling,
        place=place,
        weights=weights,
        scratch=[
            pltpu.VMEM((tokens, feats), BF16),
            pltpu.VMEM((STRIPS, words, feats // STRIPS), BF16),
            pltpu.VMEM((words, tokens), F32),
            pltpu.SemaphoreType.DMA((STRIPS,)),
        ],
        mib=22,
    )


def total(parts):
    parts = list(parts)
    while len(parts) > 1:
        parts = [a + b for a, b in zip(parts[::2], parts[1::2])]
    return parts[0]


def merge(parts):
    peak = functools.reduce(jnp.maximum, [p[0:1] for p in parts])
    mass = total([p[1:2] * jnp.exp(p[0:1] - peak) for p in parts])
    return peak, mass, total([p[2:3] for p in parts])


def pair_kernel(mine, other, out):
    merged = merge([mine[...], other[...]])
    for copy in range(out.shape[0]):
        for row in range(3):
            out[copy, row : row + 1] = merged[row]


def chips_kernel(parts, out):
    merged = merge([parts[i] for i in range(parts.shape[0])])
    for copy in range(out.shape[0]):
        for row in range(3):
            out[copy, row : row + 1] = merged[row]


def planes_kernel(parts, out):
    for group in range(2):
        peak, mass, label = merge([parts[4 * group + i] for i in range(4)])
        out[group : group + 1] = peak + jnp.log(mass)
    out[2:3] = label


def grads_kernel(place_ref, weights, grads, extra, keep, send, turned, held, sems):
    core = place_ref[0]
    tokens = grads.shape[1]
    chips, _, wide = keep.shape
    copies = strips_of(weights, held, sems)
    turned[...] = grads[...].T
    per_strip = chips // STRIPS
    for chip in range(chips):
        strip, at = chip // per_strip, (chip % per_strip) * 2 * wide
        if at == 0:
            copies[strip].wait()
        full = jnp.dot(
            turned[...], held[strip, :, at : at + 2 * wide], preferred_element_type=F32
        )
        low = full[:, :wide]
        high = full[:, wide:]
        keep[chip, :tokens] = jnp.where(core == 0, low, high)
        send[chip, :tokens] = jnp.where(core == 0, high, low)
        keep[chip, tokens:] = extra[...]
        send[chip, tokens:] = extra[...]


def split_grads(place, weights, grads, extra):
    words, tokens = grads.shape
    feats = weights.shape[1]
    wide = extra.shape[1]
    part = jax.ShapeDtypeStruct((feats // (2 * wide), tokens + EXTRA, wide), F32)
    return vmem_call(
        grads_kernel,
        [part] * 2,
        grads,
        extra,
        place=place,
        weights=weights,
        scratch=[
            pltpu.VMEM((tokens, words), BF16),
            pltpu.VMEM((STRIPS, words, feats // STRIPS), BF16),
            pltpu.SemaphoreType.DMA((STRIPS,)),
        ],
        mib=22,
    )


def line_total(parts):
    return (parts[0] + parts[2]) + (parts[1] + parts[3])


def pair_sum_kernel(x_first, place_ref, keep, got, stay, right, left, ahead, behind):
    y, x = place_ref[2], place_ref[3]
    rows = keep.shape[1] - EXTRA
    extra = keep[0, rows:] + got[0, rows:]
    for first in range(4):
        for second in range(4):
            kx, ky = (first, second) if x_first else (second, first)
            chip = lax.rem(y + ky, 4) * 4 + lax.rem(x + kx, 4)
            if first == 2:
                out, slot = (ahead, second) if second < 2 else (behind, second - 2)
            else:
                out, slot = (stay, right, None, left)[first], second
            at = slice(slot * rows, (slot + 1) * rows)
            out[at] = keep[chip, :rows] + got[chip, :rows]
    stay[4 * rows :] = extra
    ahead[2 * rows :] = extra


def relay_kernel(stay, right, left, ahead, behind, to_right, to_left):
    rows = right.shape[0]
    half = rows // 2
    to_right[:half] = right[:half] + ahead[:half]
    to_right[half:rows] = right[half:]
    to_right[rows : rows + EXTRA] = stay[rows:]
    to_right[rows + EXTRA :] = ahead[half:]
    to_left[:half] = left[:half]
    to_left[half:rows] = left[half:] + behind[...]
    to_left[rows:] = stay[rows:]


def line_sum_kernel(stay, from_left, from_right, *outs):
    rows = outs[0].shape[0] - EXTRA
    end = 4 * rows
    near = from_left[end : end + EXTRA] + from_right[end:]
    extra = (stay[end:] + from_left[end + EXTRA :]) + near
    for k, out in enumerate(outs):
        at = slice(k * rows, (k + 1) * rows)
        out[:rows] = stay[at] + (from_left[at] + from_right[at])
        out[rows:] = extra


def last_split_kernel(a0, a1, a2, a3, b0, b1, b2, b3, out):
    halves = ((a0, a1, a2, a3), (b0, b1, b2, b3))
    rows = a0.shape[0] - EXTRA
    part = rows // 4
    tails = [line_total([p[rows:] for p in half]) for half in halves]
    for plane in range(8):
        at = slice((plane % 4) * part, (plane % 4 + 1) * part)
        out[plane, :part] = line_total([p[at] for p in halves[plane // 4]])
        out[plane, part : part + EXTRA] = tails[0]
        out[plane, part + EXTRA :] = tails[1]


def moved(part, axis, step):
    return lax.ppermute(part, axis, [(i, (i + step) % 4) for i in range(4)])


def shards(hidden, head_weight, labels, loss_mask):
    weights = pltpu.with_memory_space_constraint(head_weight[0], pltpu.HBM)
    words, feats = weights.shape
    place = jnp.stack([lax.axis_index(a) for a in ("core", "tok", "y", "x")]).astype(jnp.int32)
    first_word = lax.axis_index(("y", "x", "core", "tok")) * words
    word_ids = first_word + lax.broadcasted_iota(jnp.int32, (words, 1), 0)
    mask = loss_mask.astype(F32)

    block = hidden[0]
    rows, wide = block.shape
    half = 2 * rows
    array = jax.ShapeDtypeStruct
    turns = [
        lax.ppermute(block, "tok", [(i, (i + k) % 4) for i in range(4)]) for k in range(1, 4)
    ]
    own = vmem_call(
        order_tok_kernel,
        array((16, 2 * half, wide), BF16),
        block,
        *turns,
        place=place,
        scratch=[pltpu.VMEM((4, rows, wide), BF16)],
    )
    own = exchanged(own, CHIPS)
    sibling = swapped(own, "core")
    own_z, sent = [], []
    for c in range(2):
        own_z.append(scores(place, weights, own, sibling, c))
        sent.append(lax.ppermute(own_z[c], "grp", [(0, 1)]))
        if c == 0:
            sibling, own_z[0] = lax.optimization_barrier((sibling, own_z[0]))

    hits = [word_ids == labels[c * half : (c + 1) * half][None, :] for c in range(2)]
    stats = []
    for c in range(2):
        z = own_z[c].astype(F32)
        peak = jnp.max(z, axis=0)
        stats.append(
            jnp.stack(
                [
                    peak,
                    jnp.sum(jnp.exp(z - peak), axis=0),
                    jnp.sum(jnp.where(hits[c], z, 0.0), axis=0),
                ]
            )
        )
    stats = jnp.concatenate(stats, axis=1)
    stats = vmem_call(
        pair_kernel, array((16,) + stats.shape, F32), stats, swapped(stats, "core")
    )
    stats = vmem_call(
        chips_kernel, array((8,) + stats.shape[1:], F32), exchanged(stats, CHIPS)
    )
    norms = vmem_call(planes_kernel, array(stats.shape[1:], F32), exchanged(stats, PLANES))
    norms, sent[0], sent[1] = lax.optimization_barrier((norms, sent[0], sent[1]))
    teacher_norm, student_norm, label_logit = norms

    parts = []
    for c in range(2):
        span = slice(c * half, (c + 1) * half)
        teacher_logp = sent[c].astype(F32) - teacher_norm[span]
        student_logp = own_z[c].astype(F32) - student_norm[span]
        teacher_prob = jnp.exp(teacher_logp)
        student_prob = jnp.exp(student_logp)
        diverge = jnp.sum(teacher_prob * (teacher_logp - student_logp), axis=0)
        grads = (
            (2.0 * student_prob - teacher_prob - hits[c].astype(F32)) * mask[span]
        ).astype(BF16)
        extra = jnp.zeros((EXTRA, wide), F32).at[:2].set(diverge.reshape(2, wide))
        parts.append(split_grads(place, weights, grads, extra))
    orders = (("x", "y"), ("y", "x"))
    arrays = lambda *heights: [array((height, wide), F32) for height in heights]
    full, edge = 4 * half, EXTRA
    pieces = [
        vmem_call(
            functools.partial(pair_sum_kernel, c == 0),
            arrays(full + edge, full, full, full // 2 + edge, full // 2),
            keep,
            swapped(send, "core"),
            place=place,
        )
        for c, (keep, send) in enumerate(parts)
    ]
    relayed = []
    for c, (stay, right, left, ahead, behind) in enumerate(pieces):
        axis = orders[c][0]
        relayed.append(
            vmem_call(
                relay_kernel,
                arrays(full + 2 * edge, full + edge),
                stay,
                right,
                left,
                moved(ahead, axis, 1),
                moved(behind, axis, 3),
            )
        )
    lines = []
    for c, (to_right, to_left) in enumerate(relayed):
        axis = orders[c][0]
        lines.append(
            vmem_call(
                line_sum_kernel,
                arrays(*[half + edge] * 4),
                pieces[c][0],
                moved(to_right, axis, 1),
                moved(to_left, axis, 3),
            )
        )
    pieces = [
        [lines[c][0]] + [moved(lines[c][k], orders[c][1], k) for k in range(1, 4)]
        for c in range(2)
    ]

    part = half // 4
    last = vmem_call(
        last_split_kernel,
        array((8, part + 2 * EXTRA, wide), F32),
        *pieces[0],
        *pieces[1],
    )
    mine = total(list(exchanged(last, PLANES))[4:])
    input_grads = mine[:part].astype(BF16)
    diverged = jnp.concatenate([mine[part : part + 2], mine[part + EXTRA : part + EXTRA + 2]])
    token_loss = mask * (diverged.reshape(-1) + student_norm - label_logit)
    return (input_grads, token_loss, jnp.stack([teacher_norm, student_norm]))


def solution(mesh):
    fine = Mesh(mesh.devices.reshape(2, 4, 4, 2, 4), ("grp", "y", "x", "core", "tok"))
    vocab = ("y", "x", "core")
    return jax.shard_map(
        shards,
        mesh=fine,
        in_specs=(
            P("grp", "tok", vocab),
            P("grp", vocab + ("tok",), None),
            P(),
            P(),
        ),
        out_specs=(P(("grp", "tok"), vocab), P(), P()),
        check_vma=False,
    )
```

```python
import functools
import jax
import jax.numpy as jnp
from jax import lax
from jax.experimental import pallas as pl
from jax.experimental.pallas import tpu as pltpu
from jax.sharding import Mesh, PartitionSpec as P

BF16 = jnp.bfloat16
F32 = jnp.float32
MIB = 1024 * 1024
EXTRA = 8
STRIPS = 4
CHIPS = ("y", "x")
PLANES = ("grp", "tok")


def in_vmem():
    return pl.BlockSpec(memory_space=pltpu.VMEM)


def in_smem():
    return pl.BlockSpec(memory_space=pltpu.SMEM)


def vmem_call(kernel, out_shape, *arrays, place=None, weights=None, scratch=(), mib=12):
    scalars = [] if place is None else [place]
    remote = [] if weights is None else [weights]
    return pl.pallas_call(
        kernel,
        out_shape=out_shape,
        in_specs=[in_smem()] * len(scalars)
        + [pl.BlockSpec(memory_space=pltpu.HBM)] * len(remote)
        + [in_vmem()] * len(arrays),
        out_specs=jax.tree.map(lambda _: in_vmem(), out_shape),
        scratch_shapes=list(scratch),
        compiler_params=pltpu.CompilerParams(vmem_limit_bytes=mib * MIB),
    )(*scalars, *remote, *arrays)


def swapped(x, axis):
    return lax.ppermute(x, axis, [(0, 1), (1, 0)])


def exchanged(x, axes):
    return lax.all_to_all(x, axes, 0, 0)


def order_tok_kernel(place_ref, p0, p1, p2, p3, out, held):
    me = place_ref[1]
    rows = p0.shape[0]
    for k, piece in enumerate((p0, p1, p2, p3)):
        held[lax.rem(me + 4 - k, 4)] = piece[...]
    for chip in range(out.shape[0]):
        for j in range(4):
            out[chip, j * rows : (j + 1) * rows] = held[j]


def strips_of(weights, held, sems):
    depth = held.shape[2]
    copies = [
        pltpu.make_async_copy(weights.at[:, pl.ds(i * depth, depth)], held.at[i], sems.at[i])
        for i in range(STRIPS)
    ]
    for copy in copies:
        copy.start()
    return copies


def scores_kernel(half, place_ref, weights, own, sibling, out, joined, held, acc, sems):
    core = place_ref[0]
    chips, _, wide = own.shape
    tokens = out.shape[1]
    rows = slice(half * tokens, (half + 1) * tokens)
    depth = held.shape[2]
    words = out.shape[0]
    copies = strips_of(weights, held, sems)

    def join(first, second):
        for chip in range(chips):
            at = 2 * chip * wide
            joined[:, at : at + wide] = first[chip, rows]
            joined[:, at + wide : at + 2 * wide] = second[chip, rows]

    @pl.when(core == 0)
    def _():
        join(own, sibling)

    @pl.when(core != 0)
    def _():
        join(sibling, own)

    tall = 608
    for i in range(STRIPS):
        copies[i].wait()
        for start in range(0, words, tall):
            at = slice(start, min(start + tall, words))
            part = lax.dot_general(
                held[i, at],
                joined[:, i * depth : (i + 1) * depth],
                (((1,), (1,)), ((), ())),
                preferred_element_type=F32,
            )
            if i > 0:
                part = acc[at] + part
            if i < STRIPS - 1:
                acc[at] = part
            else:
                out[at] = part.astype(BF16)


def scores(place, weights, own, sibling, half):
    words, feats = weights.shape
    tokens = own.shape[1] // 2
    return vmem_call(
        functools.partial(scores_kernel, half),
        jax.ShapeDtypeStruct((words, tokens), BF16),
        own,
        sibling,
        place=place,
        weights=weights,
        scratch=[
            pltpu.VMEM((tokens, feats), BF16),
            pltpu.VMEM((STRIPS, words, feats // STRIPS), BF16),
            pltpu.VMEM((words, tokens), F32),
            pltpu.SemaphoreType.DMA((STRIPS,)),
        ],
        mib=22,
    )


def total(parts):
    parts = list(parts)
    while len(parts) > 1:
        parts = [a + b for a, b in zip(parts[::2], parts[1::2])]
    return parts[0]


def merge(parts):
    peak = functools.reduce(jnp.maximum, [p[0:1] for p in parts])
    mass = total([p[1:2] * jnp.exp(p[0:1] - peak) for p in parts])
    return peak, mass, total([p[2:3] for p in parts])


def pair_kernel(mine, other, out):
    merged = merge([mine[...], other[...]])
    for copy in range(out.shape[0]):
        for row in range(3):
            out[copy, row : row + 1] = merged[row]


def chips_kernel(parts, out):
    merged = merge([parts[i] for i in range(parts.shape[0])])
    for copy in range(out.shape[0]):
        for row in range(3):
            out[copy, row : row + 1] = merged[row]


def planes_kernel(parts, out):
    for group in range(2):
        peak, mass, label = merge([parts[4 * group + i] for i in range(4)])
        out[group : group + 1] = peak + jnp.log(mass)
    out[2:3] = label


def grads_kernel(
    place_ref, weights, lower, upper, low_extra, high_extra, *refs
):
    keeps, sends, (turned, held, sems) = refs[:2], refs[2:4], refs[4:]
    core = place_ref[0]
    tokens = lower.shape[1]
    chips, _, wide = keeps[0].shape
    copies = strips_of(weights, held, sems)
    turned[:tokens] = lower[...].T
    turned[tokens:] = upper[...].T
    per_strip = chips // STRIPS
    for chip in range(chips):
        strip, at = chip // per_strip, (chip % per_strip) * 2 * wide
        if at == 0:
            copies[strip].wait()
        full = jnp.dot(
            turned[...], held[strip, :, at : at + 2 * wide], preferred_element_type=F32
        )
        mine = jnp.where(core == 0, full[:, :wide], full[:, wide:])
        theirs = jnp.where(core == 0, full[:, wide:], full[:, :wide])
        for half, extra in enumerate((low_extra, high_extra)):
            rows = slice(half * tokens, (half + 1) * tokens)
            keeps[half][chip, :tokens] = mine[rows]
            sends[half][chip, :tokens] = theirs[rows]
            keeps[half][chip, tokens:] = extra[...]
            sends[half][chip, tokens:] = extra[...]


def split_grads(place, weights, grads, extras):
    words, tokens = grads[0].shape
    feats = weights.shape[1]
    wide = extras[0].shape[1]
    part = jax.ShapeDtypeStruct((feats // (2 * wide), tokens + EXTRA, wide), F32)
    out = vmem_call(
        grads_kernel,
        [part] * 4,
        *grads,
        *extras,
        place=place,
        weights=weights,
        scratch=[
            pltpu.VMEM((2 * tokens, words), BF16),
            pltpu.VMEM((STRIPS, words, feats // STRIPS), BF16),
            pltpu.SemaphoreType.DMA((STRIPS,)),
        ],
        mib=28,
    )
    return [(out[0], out[2]), (out[1], out[3])]


def line_total(parts):
    return (parts[0] + parts[2]) + (parts[1] + parts[3])


def pair_sum_kernel(x_first, place_ref, keep, got, stay, right, left, ahead, behind):
    y, x = place_ref[2], place_ref[3]
    rows = keep.shape[1] - EXTRA
    extra = keep[0, rows:] + got[0, rows:]
    for first in range(4):
        for second in range(4):
            kx, ky = (first, second) if x_first else (second, first)
            chip = lax.rem(y + ky, 4) * 4 + lax.rem(x + kx, 4)
            if first == 2:
                out, slot = (ahead, second) if second < 2 else (behind, second - 2)
            else:
                out, slot = (stay, right, None, left)[first], second
            at = slice(slot * rows, (slot + 1) * rows)
            out[at] = keep[chip, :rows] + got[chip, :rows]
    stay[4 * rows :] = extra
    ahead[2 * rows :] = extra


def relay_kernel(stay, right, left, ahead, behind, to_right, to_left):
    rows = right.shape[0]
    half = rows // 2
    to_right[:half] = right[:half] + ahead[:half]
    to_right[half:rows] = right[half:]
    to_right[rows : rows + EXTRA] = stay[rows:]
    to_right[rows + EXTRA :] = ahead[half:]
    to_left[:half] = left[:half]
    to_left[half:rows] = left[half:] + behind[...]
    to_left[rows:] = stay[rows:]


def line_sum_kernel(stay, from_left, from_right, *outs):
    rows = outs[0].shape[0] - EXTRA
    end = 4 * rows
    near = from_left[end : end + EXTRA] + from_right[end:]
    extra = (stay[end:] + from_left[end + EXTRA :]) + near
    for k, out in enumerate(outs):
        at = slice(k * rows, (k + 1) * rows)
        out[:rows] = stay[at] + (from_left[at] + from_right[at])
        out[rows:] = extra


def last_split_kernel(a0, a1, a2, a3, b0, b1, b2, b3, out):
    halves = ((a0, a1, a2, a3), (b0, b1, b2, b3))
    rows = a0.shape[0] - EXTRA
    part = rows // 4
    tails = [line_total([p[rows:] for p in half]) for half in halves]
    for plane in range(8):
        at = slice((plane % 4) * part, (plane % 4 + 1) * part)
        out[plane, :part] = line_total([p[at] for p in halves[plane // 4]])
        out[plane, part : part + EXTRA] = tails[0]
        out[plane, part + EXTRA :] = tails[1]


def finish_kernel(parts, rows_out, diverged):
    mine = total([parts[i] for i in range(4, 8)])
    part = rows_out.shape[0]
    rows_out[...] = mine[:part].astype(BF16)
    diverged[:2] = mine[part : part + 2]
    diverged[2:] = mine[part + EXTRA : part + EXTRA + 2]


def moved(part, axis, step):
    return lax.ppermute(part, axis, [(i, (i + step) % 4) for i in range(4)])


def shards(hidden, head_weight, labels, loss_mask):
    weights = pltpu.with_memory_space_constraint(head_weight[0], pltpu.HBM)
    words, feats = weights.shape
    place = jnp.stack([lax.axis_index(a) for a in ("core", "tok", "y", "x")]).astype(jnp.int32)
    first_word = lax.axis_index(("y", "x", "core", "tok")) * words
    word_ids = first_word + lax.broadcasted_iota(jnp.int32, (words, 1), 0)
    mask = loss_mask.astype(F32)

    block = hidden[0]
    rows, wide = block.shape
    half = 2 * rows
    array = jax.ShapeDtypeStruct
    turns = [
        lax.ppermute(block, "tok", [(i, (i + k) % 4) for i in range(4)]) for k in range(1, 4)
    ]
    own = vmem_call(
        order_tok_kernel,
        array((16, 2 * half, wide), BF16),
        block,
        *turns,
        place=place,
        scratch=[pltpu.VMEM((4, rows, wide), BF16)],
    )
    own = exchanged(own, CHIPS)
    sibling = swapped(own, "core")
    own_z, sent = [], []
    for c in range(2):
        own_z.append(scores(place, weights, own, sibling, c))
        sent.append(lax.ppermute(own_z[c], "grp", [(0, 1)]))
        if c == 0:
            sibling, own_z[0] = lax.optimization_barrier((sibling, own_z[0]))

    hits = [word_ids == labels[c * half : (c + 1) * half][None, :] for c in range(2)]
    stats = []
    for c in range(2):
        z = own_z[c].astype(F32)
        peak = jnp.max(z, axis=0)
        stats.append(
            jnp.stack(
                [
                    peak,
                    jnp.sum(jnp.exp(z - peak), axis=0),
                    jnp.sum(jnp.where(hits[c], z, 0.0), axis=0),
                ]
            )
        )
    stats = jnp.concatenate(stats, axis=1)
    stats = vmem_call(
        pair_kernel, array((16,) + stats.shape, F32), stats, swapped(stats, "core")
    )
    stats = vmem_call(
        chips_kernel, array((8,) + stats.shape[1:], F32), exchanged(stats, CHIPS)
    )
    norms = vmem_call(planes_kernel, array(stats.shape[1:], F32), exchanged(stats, PLANES))
    norms, sent[0], sent[1] = lax.optimization_barrier((norms, sent[0], sent[1]))
    teacher_norm, student_norm, label_logit = norms

    parts = []
    for c in range(2):
        span = slice(c * half, (c + 1) * half)
        teacher_logp = sent[c].astype(F32) - teacher_norm[span]
        student_logp = own_z[c].astype(F32) - student_norm[span]
        teacher_prob = jnp.exp(teacher_logp)
        student_prob = jnp.exp(student_logp)
        diverge = jnp.sum(teacher_prob * (teacher_logp - student_logp), axis=0)
        grads = (
            (2.0 * student_prob - teacher_prob - hits[c].astype(F32)) * mask[span]
        ).astype(BF16)
        extra = jnp.zeros((EXTRA, wide), F32).at[:2].set(diverge.reshape(2, wide))
        parts.append((grads, extra))
    parts = split_grads(place, weights, *zip(*parts))
    orders = (("x", "y"), ("y", "x"))
    arrays = lambda *heights: [array((height, wide), F32) for height in heights]
    full, edge = 4 * half, EXTRA
    pieces = [
        vmem_call(
            functools.partial(pair_sum_kernel, c == 0),
            arrays(full + edge, full, full, full // 2 + edge, full // 2),
            keep,
            swapped(send, "core"),
            place=place,
        )
        for c, (keep, send) in enumerate(parts)
    ]
    relayed = []
    for c, (stay, right, left, ahead, behind) in enumerate(pieces):
        axis = orders[c][0]
        relayed.append(
            vmem_call(
                relay_kernel,
                arrays(full + 2 * edge, full + edge),
                stay,
                right,
                left,
                moved(ahead, axis, 1),
                moved(behind, axis, 3),
            )
        )
    lines = []
    for c, (to_right, to_left) in enumerate(relayed):
        axis = orders[c][0]
        lines.append(
            vmem_call(
                line_sum_kernel,
                arrays(*[half + edge] * 4),
                pieces[c][0],
                moved(to_right, axis, 1),
                moved(to_left, axis, 3),
            )
        )
    pieces = [
        [lines[c][0]] + [moved(lines[c][k], orders[c][1], k) for k in range(1, 4)]
        for c in range(2)
    ]

    part = half // 4
    last = vmem_call(
        last_split_kernel,
        array((8, part + 2 * EXTRA, wide), F32),
        *pieces[0],
        *pieces[1],
    )
    input_grads, diverged = vmem_call(
        finish_kernel,
        [array((part, wide), BF16), array((4 * rows // wide, wide), F32)],
        exchanged(last, PLANES),
    )
    token_loss = mask * (diverged.reshape(-1) + student_norm - label_logit)
    return (input_grads, token_loss, jnp.stack([teacher_norm, student_norm]))


def solution(mesh):
    fine = Mesh(mesh.devices.reshape(2, 4, 4, 2, 4), ("grp", "y", "x", "core", "tok"))
    vocab = ("y", "x", "core")
    return jax.shard_map(
        shards,
        mesh=fine,
        in_specs=(
            P("grp", "tok", vocab),
            P("grp", vocab + ("tok",), None),
            P(),
            P(),
        ),
        out_specs=(P(("grp", "tok"), vocab), P(), P()),
        check_vma=False,
    )
```
